32 devices in a mesh: dp: 16 (over z, x, core), shard: 2 (over y).
Axes of the slice: x: 2, y: 2, z: 4, core: 2. Of those that a mesh axis runs over, the one named last changes fastest.
Arguments:
- inputs: bfloat16 [32, 8, 8, 8, 256], P(('dp', 'shard')), may hold values from -6 to 6
- cotangent: bfloat16 [32, 4, 4, 4, 256], P(('dp', 'shard')), may hold values from -6 to 6
- weights: bfloat16 [28, 256, 256], P(None, 'shard'), may hold values from -0.078125 to 0.078125
Outputs:
- outputs: bfloat16 [32, 4, 4, 4, 256], P(('dp', 'shard'))
- input_grad: bfloat16 [32, 8, 8, 8, 256], P(('dp', 'shard'))
- weight_grad: float32 [28, 256, 256], P(None, 'shard')
The draws below stay inside these ranges and needn't reach their ends.
All inputs are finite; a program needn't handle non-finite values.
Results may differ from the reference program's by a relative error of at most 0.012.
Values may be sent and summed in bfloat16 or wider, within the bound.
No kernel may reach another device: no remote copies, remote signals or barrier semaphores. Data moves between devices by JAX's collectives and lax.ppermute only.
A program may use at most 64 MiB of HBM per device.

```python
import jax
import jax.numpy as jnp
from jax import lax

C = 256
TAPS = 28
P_SIZE = 8
Q = 4
SAMPLES = 32


def strengthened(array, rng, source, target, shards_of, factor):
    owner, partner = [(jnp.arange(array.shape[position]) // (array.shape[position] // shards_of)).reshape([-1 if axis == position else 1 for axis in range(array.ndim)]) for position in (source, target)]
    chosen = jax.random.permutation(rng, shards_of)[partner]
    strong = (owner == chosen) | (owner == (partner + shards_of // 2) % shards_of)
    return jnp.where(strong, factor * array, array)


def steps_of(own_key, dims, cuts, smallest, high):
    def one(position, blocks):
        heights = jax.random.uniform(jax.random.fold_in(jax.random.fold_in(own_key, 6), position), (blocks,), jnp.float32, smallest / len(cuts), high / len(cuts))
        return jnp.repeat(jnp.exp(heights), dims[position] // blocks).reshape((-1,) + (1,) * (len(dims) - position - 1))

    loudness = one(*cuts[0])
    for cut in cuts[1:]:
        loudness = loudness * one(*cut)
    return loudness


def normal_values(rng, extent, deviation, limit, split=(), held_as=jnp.bfloat16):
    gain = steps_of(rng, extent, split, -0.22, 0.18) if split else 1.0
    entries = jax.random.normal(rng, extent, jnp.float32) * deviation * gain
    return jnp.minimum(jnp.maximum(entries, -limit), limit).astype(held_as)


def gaussian_with(own_key, extent, spread, bound, split, heavy, held_as=jnp.bfloat16):
    array = spread * jax.random.normal(own_key, extent, jnp.float32)
    if split:
        array = array * steps_of(own_key, extent, split, -0.22, 0.18)
    return jnp.clip(strengthened(array, jax.random.fold_in(own_key, 3), *heavy), -bound, bound).astype(held_as)


def setup_inputs(seed: int = 0) -> dict:
    arg_keys = jax.random.split(jax.random.key(seed), 4)
    inputs = gaussian_with(arg_keys[0], (SAMPLES, P_SIZE, P_SIZE, P_SIZE, C), 1.0, 6.0, ((0, 32),), (0, 4, 32, 2.75))
    cotangent = normal_values(arg_keys[1], (SAMPLES, Q, Q, Q, C), 1.0, 6.0, ((0, 32),))
    weights = normal_values(arg_keys[2], (TAPS, C, C), (27 * C) ** -0.5, 0.078125, ((1, 2),))
    return {"inputs": inputs, "cotangent": cotangent, "weights": weights}


def one_sample(inputs, cotangent, flat_weights):
    edge = inputs.shape[0]
    half = edge // 2
    chans = inputs.shape[3]
    act = jax.nn.silu(inputs.astype(jnp.float32)).astype(jnp.bfloat16)
    padded = jnp.pad(act, ((1, 1), (1, 1), (1, 1), (0, 0)))
    pieces = []
    for first in range(3):
        for second in range(3):
            for third in range(3):
                pieces.append(padded[first:first + 2 * half:2, second:second + 2 * half:2, third:third + 2 * half:2])
    pieces.append(inputs[0::2, 0::2, 0::2])
    cols = jnp.stack(pieces, axis=3).reshape(half * half * half, 28 * chans)
    outputs = jnp.dot(cols, flat_weights, preferred_element_type=jnp.float32).astype(jnp.bfloat16)
    grad_rows = cotangent.reshape(half * half * half, chans)
    dcols = jnp.dot(grad_rows, flat_weights.T, preferred_element_type=jnp.float32).reshape(half, half, half, 28, chans)
    grid = jnp.zeros((edge + 2, edge + 2, edge + 2, chans), jnp.float32)
    for first in range(3):
        for second in range(3):
            for third in range(3):
                grid = grid.at[first:first + 2 * half:2, second:second + 2 * half:2, third:third + 2 * half:2].add(dcols[:, :, :, 9 * first + 3 * second + third])
    values = inputs.astype(jnp.float32)
    sigma = jax.nn.sigmoid(values)
    grad_in = grid[1:-1, 1:-1, 1:-1] * sigma * (1.0 + values * (1.0 - sigma))
    grad_in = grad_in.at[0::2, 0::2, 0::2].add(dcols[:, :, :, 27])
    sample_grad = jnp.dot(cols.T, grad_rows, preferred_element_type=jnp.float32).astype(jnp.bfloat16)
    return outputs.reshape(half, half, half, chans), grad_in.astype(jnp.bfloat16), sample_grad


def reference(inputs, cotangent, weights):
    flat_weights = weights.reshape(TAPS * C, C)

    def step(total, pair):
        outputs, grad_in, sample_grad = one_sample(pair[0], pair[1], flat_weights)
        return total + sample_grad.astype(jnp.float32), (outputs, grad_in)

    start = jnp.zeros((TAPS * C, C), jnp.float32)
    total, (outputs, input_grad) = lax.scan(step, start, (inputs, cotangent))
    return outputs, input_grad, total.reshape(TAPS, C, C)
```

```python
import functools

import jax
import jax.numpy as jnp
from jax import lax
from jax.experimental import pallas as pl
from jax.experimental.pallas import tpu as pltpu
from jax.sharding import PartitionSpec as P

LANES = 128
PARTS = 8
VMEM_BYTES = 48 * 1024 * 1024
BF16 = jnp.bfloat16
F32 = jnp.float32

TAP_CLASS = (1, 0, 1)
TAP_SHIFT = (1, 0, 0)


def tap_table():
    table = []
    for first in range(3):
        for second in range(3):
            for third in range(3):
                taps = (first, second, third)
                table.append(
                    (tuple(TAP_CLASS[t] for t in taps), tuple(TAP_SHIFT[t] for t in taps))
                )
    return table


def class_index(parity):
    return 4 * parity[0] + 2 * parity[1] + parity[2]


def dot(left, right, contract=(1, 0)):
    return lax.dot_general(
        left, right, (((contract[0],), (contract[1],)), ((), ())), preferred_element_type=F32
    )


def row_digits(rows, half):
    row = lax.broadcasted_iota(jnp.int32, (rows, 1), 0)
    return (row // (half * half)) % half, (row // half) % half, row % half


def shift_rows(value, shift, half, forward):
    if not any(shift):
        return value
    rows = value.shape[0]
    offset = (shift[0] * half + shift[1]) * half + shift[2]
    keep = None
    for digit, step in zip(row_digits(rows, half), shift):
        if step:
            inside = digit >= step if forward else digit < half - step
            keep = inside if keep is None else keep & inside
    moved = pltpu.roll(value, offset if forward else rows - offset, 0)
    return jnp.where(keep, moved, 0.0)


def plane_order(edge, blocks):
    half = edge // 2
    plane = edge * edge
    size = blocks * plane
    row = lax.broadcasted_iota(jnp.int32, (size, size), 0)
    col = lax.broadcasted_iota(jnp.int32, (size, size), 1)
    inner = row % plane
    parity, cell = inner // (half * half), inner % (half * half)
    second = 2 * (cell // half) + parity // 2
    third = 2 * (cell % half) + parity % 2
    return (col == (row // plane) * plane + second * edge + third).astype(BF16)


def pack_kernel(edge, shards_of, parts, x_ref, cot_ref, pieces_ref, send_ref, own_ref):
    half = edge // 2
    hh, cells, plane = half * half, half**3, edge * edge
    groups = parts // 2
    width = LANES // groups
    here = lax.axis_index("shard")
    blocks = 256 // plane
    order = plane_order(edge, blocks)
    planes = []
    for start in range(0, edge, blocks):
        part = x_ref[start * plane : (start + blocks) * plane, :]
        moved = dot(order, part).astype(BF16)
        planes += [moved[b * plane : (b + 1) * plane] for b in range(blocks)]
    classes = []
    for first in range(2):
        for inner in range(4):
            classes.append(
                jnp.concatenate(
                    [planes[2 * i + first][inner * hh : (inner + 1) * hh] for i in range(half)], axis=0
                )
            )
    size = 4 * LANES
    row = lax.broadcasted_iota(jnp.int32, (size, size), 0)
    col = lax.broadcasted_iota(jnp.int32, (size, size), 1)
    source = ((col // width) % 4) * LANES + (col // LANES) * width + col % width
    lane_order = (row == source).astype(BF16)
    for owner in range(shards_of):
        lanes = slice(owner * LANES, (owner + 1) * LANES)
        wide = jnp.concatenate(
            [
                jnp.concatenate([classes[4 * first + inner][:, lanes] for inner in range(4)], axis=1)
                for first in range(2)
            ],
            axis=0,
        )
        packed = dot(wide, lane_order).astype(BF16)
        for part in range(parts):
            group, side = part // 2, part % 2
            piece = part * shards_of + owner
            pieces_ref[piece, 0 : 2 * cells, :] = packed[:, group * LANES : (group + 1) * LANES]
            pieces_ref[piece, 2 * cells : 3 * cells, :] = cot_ref[:, side * LANES : (side + 1) * LANES]
    for index, value in enumerate(classes):
        low, high = value[:, :LANES], value[:, LANES:]
        own_ref[index * cells : (index + 1) * cells, :] = jnp.where(here == 0, low, high)
        send_ref[index * cells : (index + 1) * cells, :] = jnp.where(here == 0, high, low)
    for side in range(2):
        rows = slice((8 + side) * cells, (9 + side) * cells)
        own_ref[rows, :] = cot_ref[:, side * LANES : (side + 1) * LANES]
        send_ref[rows, :] = cot_ref[:, side * LANES : (side + 1) * LANES]


def weight_kernel(half, samples, width, splits, got_ref, *out_refs):
    cells = half**3
    rows = samples * cells
    acts, raw = [], None
    for first in range(2):
        value = got_ref[:, first * cells : (first + 1) * cells, :].reshape(rows, LANES)
        if first == 0:
            raw = value
        wide = value.astype(F32)
        acts.append((wide / (1.0 + jnp.exp(-wide))).astype(BF16))
    cots = got_ref[:, 2 * cells : 3 * cells, :].reshape(rows, LANES).astype(F32)
    moved = {}
    for si in range(2):
        for sj in range(2):
            for sk in range(2):
                moved[si, sj, sk] = shift_rows(cots, (si, sj, sk), half, False).astype(BF16)
    sums = {}
    for si in range(2):
        right = jnp.concatenate([moved[si, sj, sk] for sj in range(2) for sk in range(2)], axis=1)
        for first in range(si, 2):
            sums[first, si] = dot(acts[first], right, (0, 0))
    taps = []
    for parity, shift in tap_table():
        block = sums[parity[0], shift[0]]
        row = (2 * parity[1] + parity[2]) * width
        col = (2 * shift[1] + shift[2]) * LANES
        taps.append(block[row : row + width, col : col + LANES])
    taps.append(dot(raw, moved[0, 0, 0], (0, 0))[:width])
    start = 0
    for ref, count in zip(out_refs, splits):
        for index in range(count):
            ref[index] = taps[start + index].astype(BF16)
        start += count


def sample_kernel(half, own_ref, other_ref, w_ref, part_ref, grad_ref, send_ref):
    cells = half**3
    both = 2 * cells
    count = len(tap_table())

    def rows_of(index):
        rows = slice(index * cells, (index + 1) * cells)
        return jnp.concatenate([own_ref[rows, :], other_ref[rows, :]], axis=0)

    cots = jnp.concatenate([rows_of(8), rows_of(9)], axis=1).astype(F32)
    moved, gathered = {}, {}
    shifts = [(si, sj, sk) for si in range(2) for sj in range(2) for sk in range(2)]
    for shift in shifts:
        moved[shift] = shift_rows(cots, shift, half, False).astype(BF16)
    for index in range(8):
        value = rows_of(index)
        wide = value.astype(F32)
        sigma = 1.0 / (1.0 + jnp.exp(-wide))
        act = (wide * sigma).astype(BF16)
        back = None
        for tap, (parity, shift) in enumerate(tap_table()):
            if class_index(parity) != index:
                continue
            weight = w_ref[tap]
            term = dot(act, weight)
            gathered[shift] = term if shift not in gathered else gathered[shift] + term
            term = dot(moved[shift], weight, (1, 1))
            back = term if back is None else back + term
        grad = back * sigma * (1.0 + wide * (1.0 - sigma))
        if index == 0:
            weight = w_ref[count]
            gathered[0, 0, 0] = gathered[0, 0, 0] + dot(value, weight)
            grad = grad + dot(moved[0, 0, 0], weight, (1, 1))
        grad = grad.astype(BF16)
        rows = slice(index * cells, (index + 1) * cells)
        grad_ref[rows, :] = grad[:cells]
        send_ref[rows, :] = grad[cells:]
    total = gathered[0, 0, 0]
    for shift in shifts[1:]:
        total = total + shift_rows(gathered[shift], shift, half, True)
    part_ref[...] = total[:cells]
    for side in range(2):
        send_ref[(8 + side) * cells : (9 + side) * cells, :] = total[
            cells:both, side * LANES : (side + 1) * LANES
        ].astype(BF16)


def finish_kernel(edge, part_ref, grad_ref, got_ref, out_ref, back_ref):
    half = edge // 2
    hh, cells, plane = half * half, half**3, edge * edge
    here = lax.axis_index("shard")
    got = jnp.concatenate(
        [got_ref[8 * cells : 9 * cells, :], got_ref[9 * cells : 10 * cells, :]], axis=1
    )
    out_ref[...] = (part_ref[...] + got.astype(F32)).astype(BF16)
    mine, theirs = grad_ref[...], got_ref[0 : 8 * cells, :]
    wide = jnp.concatenate(
        [jnp.where(here == 0, mine, theirs), jnp.where(here == 0, theirs, mine)], axis=1
    )
    blocks = 256 // plane
    order = plane_order(edge, blocks)
    for start in range(0, edge, blocks):
        pieces = []
        for b in range(blocks):
            first, i = (start + b) % 2, (start + b) // 2
            for inner in range(4):
                row = (4 * first + inner) * cells + i * hh
                pieces.append(wide[row : row + hh])
        back_ref[start * plane : (start + blocks) * plane, :] = dot(
            order, jnp.concatenate(pieces, axis=0), (0, 0)
        ).astype(BF16)


def place_kernel(parts, width, block, has_base, *refs):
    piece_refs, out_ref = refs[has_base : has_base + parts], refs[-1]
    part = lax.rem(lax.axis_index("dp"), parts)
    step = pl.program_id(0)
    for distance, ref in enumerate(piece_refs):
        owner = part ^ distance
        group, side = owner // 2, lax.rem(owner, 2)
        rows = pl.ds(pl.multiple_of(group * width, width), width)
        cols = pl.ds(pl.multiple_of(side * LANES, LANES), LANES)
        out_ref[:, rows, cols] = ref[pl.ds(step * block, block)].astype(F32)


def vmem_call(body, outs, flops=0, **kwargs):
    space = pl.BlockSpec(memory_space=pltpu.VMEM)
    return pl.pallas_call(
        body,
        out_shape=outs,
        out_specs=jax.tree.map(lambda _: space, outs),
        compiler_params=pltpu.CompilerParams(vmem_limit_bytes=VMEM_BYTES),
        cost_estimate=pl.CostEstimate(flops=flops, bytes_accessed=1 << 20, transcendentals=0),
        **kwargs,
    )


def shape(dims, dtype=BF16):
    return jax.ShapeDtypeStruct(dims, dtype)


def shards(groups_of, shards_of, inputs, cotangent, weights):
    edge, chans = inputs.shape[1], inputs.shape[4]
    half = edge // 2
    cells = half**3
    count, own_chans = weights.shape[0], weights.shape[1]
    parts = PARTS
    samples = parts * shards_of
    width = LANES // (parts // 2)
    values = inputs.reshape(edge**3, chans)
    rows = cotangent.reshape(cells, chans)

    pieces, send, own = vmem_call(
        functools.partial(pack_kernel, edge, shards_of, parts),
        (shape((samples, 3 * cells, LANES)), shape((10 * cells, LANES)), shape((10 * cells, LANES))),
    )(values, rows)
    got = lax.all_to_all(
        pieces,
        ("dp", "shard"),
        split_axis=0,
        concat_axis=0,
        tiled=True,
        axis_index_groups=[
            [start + i for i in range(samples)] for start in range(0, groups_of * shards_of, samples)
        ],
    )
    other = lax.ppermute(send, "shard", [(0, 1), (1, 0)])

    def across(value, distance):
        return lax.ppermute(value, "dp", [(i, i ^ distance) for i in range(groups_of)])

    splits = (count // 2, count - count // 2)
    sums = vmem_call(
        functools.partial(weight_kernel, half, samples, width, splits),
        tuple(shape((n, width, LANES)) for n in splits),
    )(got)
    if not isinstance(sums, (tuple, list)):
        sums = (sums,)

    part, grad, back = vmem_call(
        functools.partial(sample_kernel, half),
        (shape((cells, chans), F32), shape((8 * cells, LANES)), shape((10 * cells, LANES))),
    )(own, other, weights)
    returned = lax.ppermute(back, "shard", [(0, 1), (1, 0)])
    outputs, input_grad = vmem_call(
        functools.partial(finish_kernel, edge),
        (shape((cells, chans)), shape((edge**3, chans))),
    )(part, grad, returned)

    block = count // 4
    base = None
    start = 0
    for total, n in zip(sums, splits):
        distance = parts
        while distance < groups_of:
            total = (total.astype(F32) + across(total, distance).astype(F32)).astype(BF16)
            distance *= 2
        held = {0: total}
        for distance in range(2, parts, 2):
            held[distance] = across(total, distance)
        for distance in range(0, parts, 2):
            held[distance + 1] = across(held[distance], 1)
        args = [held[i] for i in range(parts)]
        whole = pl.BlockSpec(memory_space=pltpu.VMEM)
        first = start // block
        base = pl.pallas_call(
            functools.partial(place_kernel, parts, width, block, int(base is not None)),
            grid=(n // block,),
            in_specs=([pl.BlockSpec(memory_space=pl.ANY)] if base is not None else []) + [whole] * parts,
            out_specs=pl.BlockSpec(
                (block, own_chans, chans), functools.partial(lambda first, i: (first + i, 0, 0), first)
            ),
            out_shape=shape((count, own_chans, chans), F32),
            input_output_aliases={0: 0} if base is not None else {},
            compiler_params=pltpu.CompilerParams(vmem_limit_bytes=VMEM_BYTES),
        )(*([base] if base is not None else []), *args)
        start += n
    return outputs.reshape(cotangent.shape), input_grad.reshape(inputs.shape), base


def build_cols(values):
    edge = values.shape[0]
    half = edge // 2
    width = values.shape[3]
    act = jax.nn.silu(values.astype(jnp.float32)).astype(jnp.bfloat16)
    padded = jnp.pad(act, ((1, 1), (1, 1), (1, 1), (0, 0)))
    pieces = []
    for first in range(3):
        for second in range(3):
            for third in range(3):
                pieces.append(
                    padded[
                        first : first + edge : 2,
                        second : second + edge : 2,
                        third : third + edge : 2,
                    ]
                )
    pieces.append(values[0::2, 0::2, 0::2])
    return jnp.stack(pieces, axis=3).reshape(half * half * half, 28, width)


def spread_back(values, grad_rows, piece, half):
    width = piece.shape[1]
    edge = 2 * half
    grid = jnp.zeros((edge + 2, edge + 2, edge + 2, width), jnp.float32)
    for first in range(3):
        block = jnp.einsum(
            "qo,tco->qtc",
            grad_rows,
            piece[9 * first : 9 * first + 9],
            preferred_element_type=jnp.float32,
        )
        block = block.reshape(half, half, half, 9, width)
        for second in range(3):
            for third in range(3):
                grid = grid.at[
                    first : first + edge : 2, second : second + edge : 2, third : third + edge : 2
                ].add(block[:, :, :, 3 * second + third])
    direct = jnp.einsum(
        "qo,co->qc", grad_rows, piece[27], preferred_element_type=jnp.float32
    ).reshape(half, half, half, width)
    own = values.astype(jnp.float32)
    sigma = jax.nn.sigmoid(own)
    grad_in = grid[1:-1, 1:-1, 1:-1] * sigma * (1.0 + own * (1.0 - sigma))
    grad_in = grad_in.at[0::2, 0::2, 0::2].add(direct)
    return grad_in.astype(jnp.bfloat16)


def general(inputs, cotangent, weights):
    values = inputs[0]
    edge = values.shape[0]
    half = edge // 2
    chans = values.shape[3]
    cols = build_cols(values)
    grad_rows = cotangent[0].reshape(half * half * half, chans)
    result = jnp.einsum(
        "qtc,tco->qo",
        cols,
        lax.all_gather(weights, "shard", axis=1, tiled=True),
        preferred_element_type=jnp.float32,
    )
    grad_in = spread_back(
        values, grad_rows, lax.all_gather(weights, "shard", axis=1, tiled=True), half
    )
    group_values = lax.all_to_all(inputs, "shard", split_axis=4, concat_axis=0, tiled=True)
    group_grads = lax.all_gather(cotangent, "shard", axis=0, tiled=True)
    count = group_values.shape[0]
    group_cols = jax.vmap(build_cols)(group_values)
    group_rows = group_grads.reshape(count, half * half * half, chans)
    per_sample = jnp.einsum(
        "sqtc,sqo->stco", group_cols, group_rows, preferred_element_type=jnp.float32
    )
    owned = jnp.sum(per_sample.astype(jnp.bfloat16).astype(jnp.float32), axis=0)
    weight_grad = lax.psum(owned, "dp")
    outputs = result.astype(jnp.bfloat16).reshape(1, half, half, half, chans)
    return (outputs, grad_in.reshape(1, edge, edge, edge, chans), weight_grad)


def fits(mesh, inputs, cotangent, weights):
    groups_of, shards_of = mesh.shape["dp"], mesh.shape["shard"]
    edge, chans = inputs.shape[1], inputs.shape[4]
    ratio = groups_of // PARTS
    return (
        shards_of == 2
        and chans == shards_of * LANES
        and inputs.shape[0] == groups_of * shards_of
        and inputs.shape[1:4] == (8, 8, 8)
        and groups_of % PARTS == 0
        and ratio & (ratio - 1) == 0
    )


def solution(mesh):
    rows = P(("dp", "shard"), None, None, None, None)
    kernel = P(None, "shard", None)

    def whole(inputs, cotangent, weights):
        body = general
        if fits(mesh, inputs, cotangent, weights):
            body = functools.partial(shards, mesh.shape["dp"], mesh.shape["shard"])
        return jax.shard_map(
            body,
            mesh=mesh,
            in_specs=(rows, rows, kernel),
            out_specs=(rows, rows, kernel),
            check_vma=False,
        )(inputs, cotangent, weights)

    return whole
```

```python
import functools

import jax
import jax.numpy as jnp
from jax import lax
from jax.experimental import pallas as pl
from jax.experimental.pallas import tpu as pltpu
from jax.sharding import PartitionSpec as P

LANES = 128
PARTS = 8
DELIVERY = (3, 1, 2, 0)
GATHER = (6, 4, 2)
SPLITS = (14, 14)
BLOCK = 7
ORDER = (0, 1)
DEPTH = 2
FINISH = 2
VMEM_BYTES = 48 * 1024 * 1024
BF16 = jnp.bfloat16
F32 = jnp.float32

TAP_CLASS = (1, 0, 1)
TAP_SHIFT = (1, 0, 0)


def tap_table():
    table = []
    for first in range(3):
        for second in range(3):
            for third in range(3):
                taps = (first, second, third)
                table.append(
                    (tuple(TAP_CLASS[t] for t in taps), tuple(TAP_SHIFT[t] for t in taps))
                )
    return table


def class_index(parity):
    return 4 * parity[0] + 2 * parity[1] + parity[2]


def dot(left, right, contract=(1, 0)):
    return lax.dot_general(
        left, right, (((contract[0],), (contract[1],)), ((), ())), preferred_element_type=F32
    )


def row_digits(rows, half):
    row = lax.broadcasted_iota(jnp.int32, (rows, 1), 0)
    return (row // (half * half)) % half, (row // half) % half, row % half


def shift_rows(value, shift, half, forward):
    if not any(shift):
        return value
    rows = value.shape[0]
    offset = (shift[0] * half + shift[1]) * half + shift[2]
    keep = None
    for digit, step in zip(row_digits(rows, half), shift):
        if step:
            inside = digit >= step if forward else digit < half - step
            keep = inside if keep is None else keep & inside
    moved = pltpu.roll(value, offset if forward else rows - offset, 0)
    return jnp.where(keep, moved, 0.0)


def plane_order(edge, blocks):
    half = edge // 2
    plane = edge * edge
    size = blocks * plane
    row = lax.broadcasted_iota(jnp.int32, (size, size), 0)
    col = lax.broadcasted_iota(jnp.int32, (size, size), 1)
    inner = row % plane
    parity, cell = inner // (half * half), inner % (half * half)
    second = 2 * (cell // half) + parity // 2
    third = 2 * (cell % half) + parity % 2
    return (col == (row // plane) * plane + second * edge + third).astype(BF16)


def rows_in(rows_ref, cot_ref, half):
    for i in range(half):
        for j in range(half):
            start = (i * half + j) * half
            rows_ref[start : start + half, :] = cot_ref[i, j].astype(F32)
    return rows_ref[...].astype(BF16)


def sorted_cells(edge, ref):
    half = edge // 2
    hh, plane = half * half, edge * edge
    blocks = 256 // plane
    order = plane_order(edge, blocks)
    planes = []
    for start in range(0, edge, blocks):
        moved = dot(order, ref[start * plane : (start + blocks) * plane, :]).astype(BF16)
        planes += [moved[b * plane : (b + 1) * plane] for b in range(blocks)]
    return [
        jnp.concatenate([planes[2 * i + first][inner * hh : (inner + 1) * hh] for i in range(half)], axis=0)
        for first in range(2)
        for inner in range(4)
    ]


def put_cots(ref, start, cots):
    cells = cots.shape[0]
    for side in range(2):
        ref[start + side * cells : start + (side + 1) * cells, :] = cots[:, side * LANES : (side + 1) * LANES]


def sort_kernel(edge, x_hbm, cot_hbm, send_ref, own_ref, rows_ref, x_ref, cot_ref, sems):
    half = edge // 2
    cells = half**3
    here = lax.axis_index("shard")
    copies = [
        pltpu.make_async_copy(x_hbm, x_ref, sems.at[0]),
        pltpu.make_async_copy(cot_hbm, cot_ref, sems.at[1]),
    ]
    for copy in copies:
        copy.start()
    for copy in copies:
        copy.wait()
    for index, value in enumerate(sorted_cells(edge, x_ref)):
        low, high = value[:, :LANES], value[:, LANES:]
        own_ref[index * cells : (index + 1) * cells, :] = jnp.where(here == 0, low, high)
        send_ref[index * cells : (index + 1) * cells, :] = jnp.where(here == 0, high, low)
    cots = rows_in(rows_ref, cot_ref, half)
    put_cots(own_ref, 8 * cells, cots)
    put_cots(send_ref, 8 * cells, cots)


def pack_kernel(edge, groups, own_ref, send_ref, x2_ref, cot2_ref, *refs):
    piece_refs, rows_ref = refs[:groups], refs[groups]
    half = edge // 2
    cells = half**3
    width = LANES // groups
    place = lax.axis_index("dp")
    core, group = lax.rem(place, 2), lax.rem(place // 2, groups)
    target = lax.axis_index("shard") ^ core
    samples = [
        [
            jnp.where(core == 0, own_ref[rows, :], send_ref[rows, :])
            for rows in (slice(index * cells, (index + 1) * cells) for index in range(8))
        ],
        [
            jnp.where(target == 0, value[:, :LANES], value[:, LANES:])
            for value in sorted_cells(edge, x2_ref)
        ],
    ]
    size = 4 * LANES
    row = lax.broadcasted_iota(jnp.int32, (size, size), 0)
    col = lax.broadcasted_iota(jnp.int32, (size, size), 1)
    source = ((col // width) % 4) * LANES + (col // LANES) * width + col % width
    lane_order = (row == source).astype(BF16)
    wide = jnp.concatenate(
        [
            jnp.concatenate(classes[4 * first : 4 * first + 4], axis=1)
            for classes in samples
            for first in range(2)
        ],
        axis=0,
    )
    packed = dot(wide, lane_order).astype(BF16)
    cots = rows_in(rows_ref, cot2_ref, half)
    for distance, ref in enumerate(piece_refs):
        owner = group ^ distance
        value = packed[:, (groups - 1) * LANES :]
        for index in range(groups - 1):
            value = jnp.where(owner == index, packed[:, index * LANES : (index + 1) * LANES], value)
        ref[0 : 4 * cells, :] = value
        ref[4 * cells : 6 * cells, :] = own_ref[8 * cells : 10 * cells, :]
        put_cots(ref, 6 * cells, cots)


def weight_kernel(half, groups, splits, *refs):
    got_refs, out_refs = refs[:groups], refs[groups:]
    cells = half**3
    width = LANES // groups
    core = lax.rem(lax.axis_index("dp"), 2)

    def gather(offset):
        return jnp.concatenate(
            [ref[start : start + cells, :] for ref in got_refs for start in offset], axis=0
        )

    acts, raw = [], None
    for first in range(2):
        value = gather([first * cells, (2 + first) * cells])
        if first == 0:
            raw = value
        wide = value.astype(F32)
        acts.append((wide / (1.0 + jnp.exp(-wide))).astype(BF16))
    cots = jnp.concatenate(
        [gather([(4 + side) * cells, (6 + side) * cells]) for side in range(2)], axis=1
    ).astype(F32)
    chans = 2 * LANES
    moved = {}
    for si in range(2):
        for sj in range(2):
            for sk in range(2):
                moved[si, sj, sk] = shift_rows(cots, (si, sj, sk), half, False).astype(BF16)
    sums = {}
    for si in range(2):
        right = jnp.concatenate([moved[si, sj, sk] for sj in range(2) for sk in range(2)], axis=1)
        for first in range(si, 2):
            sums[first, si] = dot(acts[first], right, (0, 0))
    taps = []
    for parity, shift in tap_table():
        block = sums[parity[0], shift[0]]
        row = (2 * parity[1] + parity[2]) * width
        col = (2 * shift[1] + shift[2]) * chans
        taps.append(block[row : row + width, col : col + chans])
    taps.append(dot(raw, moved[0, 0, 0], (0, 0))[:width])
    start = 0
    for index, count in enumerate(splits):
        keep_ref, give_ref = out_refs[2 * index], out_refs[2 * index + 1]
        for tap in range(count):
            low, high = taps[start + tap][:, :LANES], taps[start + tap][:, LANES:]
            keep_ref[tap] = jnp.where(core == 0, low, high)
            give_ref[tap] = jnp.where(core == 0, high, low).astype(BF16)
        start += count


def sample_kernel(half, own_ref, other_ref, w_ref, part_ref, grad_ref, send_ref):
    cells = half**3
    both = 2 * cells
    count = len(tap_table())

    def rows_of(index):
        rows = slice(index * cells, (index + 1) * cells)
        return jnp.concatenate([own_ref[rows, :], other_ref[rows, :]], axis=0)

    cots = jnp.concatenate([rows_of(8), rows_of(9)], axis=1).astype(F32)
    moved, gathered = {}, {}
    shifts = [(si, sj, sk) for si in range(2) for sj in range(2) for sk in range(2)]
    for shift in shifts:
        moved[shift] = shift_rows(cots, shift, half, False).astype(BF16)
    for index in range(8):
        value = rows_of(index)
        wide = value.astype(F32)
        sigma = 1.0 / (1.0 + jnp.exp(-wide))
        act = (wide * sigma).astype(BF16)
        back = None
        for tap, (parity, shift) in enumerate(tap_table()):
            if class_index(parity) != index:
                continue
            weight = w_ref[tap]
            term = dot(act, weight)
            gathered[shift] = term if shift not in gathered else gathered[shift] + term
            term = dot(moved[shift], weight, (1, 1))
            back = term if back is None else back + term
        grad = back * sigma * (1.0 + wide * (1.0 - sigma))
        if index == 0:
            weight = w_ref[count]
            gathered[0, 0, 0] = gathered[0, 0, 0] + dot(value, weight)
            grad = grad + dot(moved[0, 0, 0], weight, (1, 1))
        grad = grad.astype(BF16)
        rows = slice(index * cells, (index + 1) * cells)
        grad_ref[rows, :] = grad[:cells]
        send_ref[rows, :] = grad[cells:]
    total = gathered[0, 0, 0]
    for shift in shifts[1:]:
        total = total + shift_rows(gathered[shift], shift, half, True)
    part_ref[...] = total[:cells]
    for side in range(2):
        send_ref[(8 + side) * cells : (9 + side) * cells, :] = total[
            cells:both, side * LANES : (side + 1) * LANES
        ].astype(BF16)


def finish_kernel(edge, part_ref, grad_ref, got_ref, out_ref, back_ref, rows_ref):
    half = edge // 2
    hh, cells, plane = half * half, half**3, edge * edge
    here = lax.axis_index("shard")
    got = jnp.concatenate(
        [got_ref[8 * cells : 9 * cells, :], got_ref[9 * cells : 10 * cells, :]], axis=1
    )
    rows_ref[...] = part_ref[...] + got.astype(F32)
    for i in range(half):
        for j in range(half):
            start = (i * half + j) * half
            out_ref[i, j] = rows_ref[start : start + half, :].astype(BF16)
    mine, theirs = grad_ref[...], got_ref[0 : 8 * cells, :]
    wide = jnp.concatenate(
        [jnp.where(here == 0, mine, theirs), jnp.where(here == 0, theirs, mine)], axis=1
    )
    blocks = 256 // plane
    order = plane_order(edge, blocks)
    for start in range(0, edge, blocks):
        pieces = []
        for b in range(blocks):
            first, i = (start + b) % 2, (start + b) // 2
            for inner in range(4):
                row = (4 * first + inner) * cells + i * hh
                pieces.append(wide[row : row + hh])
        back_ref[start * plane : (start + blocks) * plane, :] = dot(
            order, jnp.concatenate(pieces, axis=0), (0, 0)
        ).astype(BF16)


def place_kernel(parts, width, block, has_base, *refs):
    piece_refs, out_ref = refs[has_base : has_base + parts], refs[-1]
    part = lax.rem(lax.axis_index("dp"), parts)
    step = pl.program_id(0)
    for distance, ref in enumerate(piece_refs):
        owner = part ^ distance
        group, side = owner // 2, lax.rem(owner, 2)
        rows = pl.ds(pl.multiple_of(group * width, width), width)
        cols = pl.ds(pl.multiple_of(side * LANES, LANES), LANES)
        out_ref[:, rows, cols] = ref[pl.ds(step * block, block)].astype(F32)


def vmem_call(body, outs, flops=0, scratch=(), **kwargs):
    space = pl.BlockSpec(memory_space=pltpu.VMEM)
    return pl.pallas_call(
        body,
        out_shape=outs,
        out_specs=jax.tree.map(lambda _: space, outs),
        scratch_shapes=scratch,
        compiler_params=pltpu.CompilerParams(vmem_limit_bytes=VMEM_BYTES),
        cost_estimate=pl.CostEstimate(flops=flops, bytes_accessed=1 << 20, transcendentals=0),
        **kwargs,
    )


def shape(dims, dtype=BF16):
    return jax.ShapeDtypeStruct(dims, dtype)


def after(value, *others):
    return lax.optimization_barrier((value, *others))[0]


def shards(groups_of, shards_of, inputs, cotangent, weights):
    edge, chans = inputs.shape[1], inputs.shape[4]
    half = edge // 2
    cells = half**3
    count, own_chans = weights.shape[0], weights.shape[1]
    parts = PARTS
    groups = parts // 2
    width = LANES // groups
    values = inputs.reshape(edge**3, chans)
    rows = cotangent.reshape(cotangent.shape[1:])
    row_buffer = [pltpu.VMEM((cells, chans), F32)]

    def across(value, distance):
        return lax.ppermute(value, "dp", [(i, i ^ distance) for i in range(groups_of)])

    def swap(value):
        return lax.ppermute(value, "shard", [(0, 1), (1, 0)])

    def deliver(value, distance):
        pairs = []
        for i in range(groups_of):
            for j in range(shards_of):
                pairs.append((i * shards_of + j, (i ^ (2 * distance)) * shards_of + (j ^ (i % 2))))
        return lax.ppermute(value, ("dp", "shard"), pairs)

    values2, rows2 = across(values, 1), across(rows, 1)
    send, own = vmem_call(
        functools.partial(sort_kernel, edge),
        (shape((10 * cells, LANES)),) * 2,
        scratch=row_buffer
        + [
            pltpu.VMEM(values.shape, BF16),
            pltpu.VMEM(rows.shape, BF16),
            pltpu.SemaphoreType.DMA((2,)),
        ],
        in_specs=[pl.BlockSpec(memory_space=pl.ANY)] * 2,
    )(values, rows)
    pieces = vmem_call(
        functools.partial(pack_kernel, edge, groups),
        (shape((8 * cells, LANES)),) * groups,
        scratch=row_buffer,
    )(own, send, values2, rows2)
    got = [deliver(pieces[distance], distance) for distance in DELIVERY]
    send = after(send, *got)
    other = swap(send)

    splits = SPLITS
    sums = vmem_call(
        functools.partial(weight_kernel, half, groups, splits),
        tuple(shape((n, width, LANES), t) for n in splits for t in (F32, BF16)),
    )(*got)
    totals = [
        (sums[2 * i] + across(sums[2 * i + 1], 1).astype(F32)).astype(BF16) for i in range(len(splits))
    ]

    part, grad, back = vmem_call(
        functools.partial(sample_kernel, half),
        (shape((cells, chans), F32), shape((8 * cells, LANES)), shape((10 * cells, LANES))),
    )(own, after(other, *totals), weights)
    returned = swap(back)
    outputs, input_grad = vmem_call(
        functools.partial(finish_kernel, edge),
        (shape(rows.shape), shape((edge**3, chans))),
        scratch=row_buffer,
    )(part, grad, returned)

    block = BLOCK
    arrivals, held = [], []
    for index in ORDER:
        total = totals[index]
        distance = parts
        while distance < groups_of:
            if len(arrivals) >= DEPTH:
                total = after(total, arrivals[-DEPTH])
            arrived = across(total, distance)
            arrivals.append(arrived)
            if len(arrivals) == FINISH:
                arrived, outputs, input_grad = lax.optimization_barrier((arrived, outputs, input_grad))
            total = (total.astype(F32) + arrived.astype(F32)).astype(BF16)
            distance *= 2
        held.append({0: total, **{distance: across(total, distance) for distance in GATHER}})
    base = None
    for turn, index in enumerate(ORDER):
        n, start = splits[index], sum(splits[:index])
        pieces = held[turn]
        for distance in (0,) + GATHER:
            value = pieces[distance]
            if base is not None and distance == GATHER[-1]:
                value = after(value, base)
            pieces[distance + 1] = across(value, 1)
        whole = pl.BlockSpec(memory_space=pltpu.VMEM)
        base = pl.pallas_call(
            functools.partial(place_kernel, parts, width, block, int(base is not None)),
            grid=(n // block,),
            in_specs=([pl.BlockSpec(memory_space=pl.ANY)] if base is not None else []) + [whole] * parts,
            out_specs=pl.BlockSpec(
                (block, own_chans, chans), functools.partial(lambda first, i: (first + i, 0, 0), start // block)
            ),
            out_shape=shape((count, own_chans, chans), F32),
            input_output_aliases={0: 0} if base is not None else {},
            compiler_params=pltpu.CompilerParams(vmem_limit_bytes=VMEM_BYTES),
        )(*([base] if base is not None else []), *(pieces[i] for i in range(parts)))
    return outputs.reshape(cotangent.shape), input_grad.reshape(inputs.shape), base


def build_cols(values):
    edge = values.shape[0]
    half = edge // 2
    width = values.shape[3]
    act = jax.nn.silu(values.astype(jnp.float32)).astype(jnp.bfloat16)
    padded = jnp.pad(act, ((1, 1), (1, 1), (1, 1), (0, 0)))
    pieces = []
    for first in range(3):
        for second in range(3):
            for third in range(3):
                pieces.append(
                    padded[
                        first : first + edge : 2,
                        second : second + edge : 2,
                        third : third + edge : 2,
                    ]
                )
    pieces.append(values[0::2, 0::2, 0::2])
    return jnp.stack(pieces, axis=3).reshape(half * half * half, 28, width)


def spread_back(values, grad_rows, piece, half):
    width = piece.shape[1]
    edge = 2 * half
    grid = jnp.zeros((edge + 2, edge + 2, edge + 2, width), jnp.float32)
    for first in range(3):
        block = jnp.einsum(
            "qo,tco->qtc",
            grad_rows,
            piece[9 * first : 9 * first + 9],
            preferred_element_type=jnp.float32,
        )
        block = block.reshape(half, half, half, 9, width)
        for second in range(3):
            for third in range(3):
                grid = grid.at[
                    first : first + edge : 2, second : second + edge : 2, third : third + edge : 2
                ].add(block[:, :, :, 3 * second + third])
    direct = jnp.einsum(
        "qo,co->qc", grad_rows, piece[27], preferred_element_type=jnp.float32
    ).reshape(half, half, half, width)
    own = values.astype(jnp.float32)
    sigma = jax.nn.sigmoid(own)
    grad_in = grid[1:-1, 1:-1, 1:-1] * sigma * (1.0 + own * (1.0 - sigma))
    grad_in = grad_in.at[0::2, 0::2, 0::2].add(direct)
    return grad_in.astype(jnp.bfloat16)


def general(inputs, cotangent, weights):
    values = inputs[0]
    edge = values.shape[0]
    half = edge // 2
    chans = values.shape[3]
    cols = build_cols(values)
    grad_rows = cotangent[0].reshape(half * half * half, chans)
    result = jnp.einsum(
        "qtc,tco->qo",
        cols,
        lax.all_gather(weights, "shard", axis=1, tiled=True),
        preferred_element_type=jnp.float32,
    )
    grad_in = spread_back(
        values, grad_rows, lax.all_gather(weights, "shard", axis=1, tiled=True), half
    )
    group_values = lax.all_to_all(inputs, "shard", split_axis=4, concat_axis=0, tiled=True)
    group_grads = lax.all_gather(cotangent, "shard", axis=0, tiled=True)
    count = group_values.shape[0]
    group_cols = jax.vmap(build_cols)(group_values)
    group_rows = group_grads.reshape(count, half * half * half, chans)
    per_sample = jnp.einsum(
        "sqtc,sqo->stco", group_cols, group_rows, preferred_element_type=jnp.float32
    )
    owned = jnp.sum(per_sample.astype(jnp.bfloat16).astype(jnp.float32), axis=0)
    weight_grad = lax.psum(owned, "dp")
    outputs = result.astype(jnp.bfloat16).reshape(1, half, half, half, chans)
    return (outputs, grad_in.reshape(1, edge, edge, edge, chans), weight_grad)


def fits(mesh, inputs, cotangent, weights):
    groups_of, shards_of = mesh.shape["dp"], mesh.shape["shard"]
    edge, chans = inputs.shape[1], inputs.shape[4]
    ratio = groups_of // PARTS
    return (
        shards_of == 2
        and chans == shards_of * LANES
        and inputs.shape[0] == groups_of * shards_of
        and inputs.shape[1:4] == (8, 8, 8)
        and groups_of % PARTS == 0
        and ratio & (ratio - 1) == 0
    )


def solution(mesh):
    rows = P(("dp", "shard"), None, None, None, None)
    kernel = P(None, "shard", None)

    def whole(inputs, cotangent, weights):
        body = general
        if fits(mesh, inputs, cotangent, weights):
            body = functools.partial(shards, mesh.shape["dp"], mesh.shape["shard"])
        return jax.shard_map(
            body,
            mesh=mesh,
            in_specs=(rows, rows, kernel),
            out_specs=(rows, rows, kernel),
            check_vma=False,
        )(inputs, cotangent, weights)

    return whole
```

```python
import functools

import jax
import jax.numpy as jnp
from jax import lax
from jax.experimental import pallas as pl
from jax.experimental.pallas import tpu as pltpu
from jax.sharding import PartitionSpec as P

LANES = 128
PARTS = 8
DELIVERY = (3, 1, 2, 0)
GATHER = (6, 4, 2)
SPLITS = (14, 14)
BLOCK = 7
ORDER = (0, 1)
SWAP = 2
SAMPLE = 1
STAGGER = True
BACK = 4
FINISH = 1
DELAY = 0
PLACE = 0
VMEM_BYTES = 48 * 1024 * 1024
BF16 = jnp.bfloat16
F32 = jnp.float32

TAP_CLASS = (1, 0, 1)
TAP_SHIFT = (1, 0, 0)


def tap_table():
    table = []
    for first in range(3):
        for second in range(3):
            for third in range(3):
                taps = (first, second, third)
                table.append(
                    (tuple(TAP_CLASS[t] for t in taps), tuple(TAP_SHIFT[t] for t in taps))
                )
    return table


def class_index(parity):
    return 4 * parity[0] + 2 * parity[1] + parity[2]


def dot(left, right, contract=(1, 0)):
    return lax.dot_general(
        left, right, (((contract[0],), (contract[1],)), ((), ())), preferred_element_type=F32
    )


def row_digits(rows, half):
    row = lax.broadcasted_iota(jnp.int32, (rows, 1), 0)
    return (row // (half * half)) % half, (row // half) % half, row % half


def shift_rows(value, shift, half, forward):
    if not any(shift):
        return value
    rows = value.shape[0]
    offset = (shift[0] * half + shift[1]) * half + shift[2]
    keep = None
    for digit, step in zip(row_digits(rows, half), shift):
        if step:
            inside = digit >= step if forward else digit < half - step
            keep = inside if keep is None else keep & inside
    moved = pltpu.roll(value, offset if forward else rows - offset, 0)
    return jnp.where(keep, moved, 0.0)


def plane_order(edge, blocks):
    half = edge // 2
    plane = edge * edge
    size = blocks * plane
    row = lax.broadcasted_iota(jnp.int32, (size, size), 0)
    col = lax.broadcasted_iota(jnp.int32, (size, size), 1)
    inner = row % plane
    parity, cell = inner // (half * half), inner % (half * half)
    second = 2 * (cell // half) + parity // 2
    third = 2 * (cell % half) + parity % 2
    return (col == (row // plane) * plane + second * edge + third).astype(BF16)


def rows_in(rows_ref, cot_ref, half):
    for i in range(half):
        for j in range(half):
            start = (i * half + j) * half
            rows_ref[start : start + half, :] = cot_ref[i, j].astype(F32)
    return rows_ref[...].astype(BF16)


def sorted_cells(edge, ref):
    half = edge // 2
    hh, plane = half * half, edge * edge
    blocks = 256 // plane
    order = plane_order(edge, blocks)
    planes = []
    for start in range(0, edge, blocks):
        moved = dot(order, ref[start * plane : (start + blocks) * plane, :]).astype(BF16)
        planes += [moved[b * plane : (b + 1) * plane] for b in range(blocks)]
    return [
        jnp.concatenate([planes[2 * i + first][inner * hh : (inner + 1) * hh] for i in range(half)], axis=0)
        for first in range(2)
        for inner in range(4)
    ]


def put_cots(ref, start, cots):
    cells = cots.shape[0]
    for side in range(2):
        ref[start + side * cells : start + (side + 1) * cells, :] = cots[:, side * LANES : (side + 1) * LANES]


def sort_kernel(edge, x_hbm, cot_hbm, send_ref, own_ref, rows_ref, x_ref, cot_ref, sems):
    half = edge // 2
    cells = half**3
    here = lax.axis_index("shard")
    copies = [
        pltpu.make_async_copy(x_hbm, x_ref, sems.at[0]),
        pltpu.make_async_copy(cot_hbm, cot_ref, sems.at[1]),
    ]
    for copy in copies:
        copy.start()
    for copy in copies:
        copy.wait()
    for index, value in enumerate(sorted_cells(edge, x_ref)):
        low, high = value[:, :LANES], value[:, LANES:]
        own_ref[index * cells : (index + 1) * cells, :] = jnp.where(here == 0, low, high)
        send_ref[index * cells : (index + 1) * cells, :] = jnp.where(here == 0, high, low)
    cots = rows_in(rows_ref, cot_ref, half)
    put_cots(own_ref, 8 * cells, cots)
    put_cots(send_ref, 8 * cells, cots)


def pack_kernel(edge, groups, own_ref, send_ref, x2_ref, cot2_ref, *refs):
    piece_refs, rows_ref = refs[:groups], refs[groups]
    half = edge // 2
    cells = half**3
    width = LANES // groups
    place = lax.axis_index("dp")
    core, group = lax.rem(place, 2), lax.rem(place // 2, groups)
    target = lax.axis_index("shard") ^ core
    samples = [
        [
            jnp.where(core == 0, own_ref[rows, :], send_ref[rows, :])
            for rows in (slice(index * cells, (index + 1) * cells) for index in range(8))
        ],
        [
            jnp.where(target == 0, value[:, :LANES], value[:, LANES:])
            for value in sorted_cells(edge, x2_ref)
        ],
    ]
    size = 4 * LANES
    row = lax.broadcasted_iota(jnp.int32, (size, size), 0)
    col = lax.broadcasted_iota(jnp.int32, (size, size), 1)
    source = ((col // width) % 4) * LANES + (col // LANES) * width + col % width
    lane_order = (row == source).astype(BF16)
    wide = jnp.concatenate(
        [
            jnp.concatenate(classes[4 * first : 4 * first + 4], axis=1)
            for classes in samples
            for first in range(2)
        ],
        axis=0,
    )
    packed = dot(wide, lane_order).astype(BF16)
    cots = rows_in(rows_ref, cot2_ref, half)
    for distance, ref in enumerate(piece_refs):
        owner = group ^ distance
        value = packed[:, (groups - 1) * LANES :]
        for index in range(groups - 1):
            value = jnp.where(owner == index, packed[:, index * LANES : (index + 1) * LANES], value)
        ref[0 : 4 * cells, :] = value
        ref[4 * cells : 6 * cells, :] = own_ref[8 * cells : 10 * cells, :]
        put_cots(ref, 6 * cells, cots)


def weight_kernel(half, groups, start, count, *refs):
    got_refs, (keep_ref, give_ref) = refs[:groups], refs[groups:]
    cells = half**3
    width = LANES // groups
    chans = 2 * LANES
    core = lax.rem(lax.axis_index("dp"), 2)
    table = tap_table()
    wanted = range(start, start + count)
    needs = {(table[tap][0][0], table[tap][1][0]) for tap in wanted if tap < len(table)}

    def gather(offset):
        return jnp.concatenate(
            [ref[start : start + cells, :] for ref in got_refs for start in offset], axis=0
        )

    raw, acts = {}, {}
    for first in range(2):
        raw[first] = gather([first * cells, (2 + first) * cells])
        wide = raw[first].astype(F32)
        acts[first] = (wide / (1.0 + jnp.exp(-wide))).astype(BF16)
    cots = jnp.concatenate(
        [gather([(4 + side) * cells, (6 + side) * cells]) for side in range(2)], axis=1
    )
    sums = {}
    for si in range(2):
        firsts = [first for first in range(2) if (first, si) in needs]
        if firsts:
            right = jnp.concatenate(
                [
                    shift_rows(cots.astype(F32), (si, sj, sk), half, False).astype(BF16)
                    for sj in range(2)
                    for sk in range(2)
                ],
                axis=1,
            )
            for first in firsts:
                sums[first, si] = dot(acts[first], right, (0, 0))
    for tap in wanted:
        if tap < len(table):
            parity, shift = table[tap]
            row = (2 * parity[1] + parity[2]) * width
            col = (2 * shift[1] + shift[2]) * chans
            value = sums[parity[0], shift[0]][row : row + width, col : col + chans]
        else:
            value = dot(raw[0], cots, (0, 0))[:width]
        low, high = value[:, :LANES], value[:, LANES:]
        keep_ref[tap - start] = jnp.where(core == 0, low, high)
        give_ref[tap - start] = jnp.where(core == 0, high, low).astype(BF16)


def sample_kernel(half, give, own_ref, w_ref, *refs):
    grad_ref = refs[-1]
    cells = half**3
    count = len(tap_table())
    cots = jnp.concatenate([own_ref[(8 + side) * cells : (9 + side) * cells, :] for side in range(2)], axis=1).astype(F32)
    moved, gathered = {}, {}
    shifts = [(si, sj, sk) for si in range(2) for sj in range(2) for sk in range(2)]
    for shift in shifts:
        moved[shift] = shift_rows(cots, shift, half, False).astype(BF16)
    for index in range(8):
        rows = slice(index * cells, (index + 1) * cells)
        value = own_ref[rows, :]
        wide = value.astype(F32)
        sigma = 1.0 / (1.0 + jnp.exp(-wide))
        act = (wide * sigma).astype(BF16)
        back = None
        for tap, (parity, shift) in enumerate(tap_table()):
            if class_index(parity) != index:
                continue
            weight = w_ref[tap]
            term = dot(act, weight)
            gathered[shift] = term if shift not in gathered else gathered[shift] + term
            term = dot(moved[shift], weight, (1, 1))
            back = term if back is None else back + term
        grad = back * sigma * (1.0 + wide * (1.0 - sigma))
        if index == 0:
            weight = w_ref[count]
            gathered[0, 0, 0] = gathered[0, 0, 0] + dot(value, weight)
            grad = grad + dot(moved[0, 0, 0], weight, (1, 1))
        grad_ref[rows, :] = grad.astype(BF16)
    total = gathered[0, 0, 0]
    for shift in shifts[1:]:
        total = total + shift_rows(gathered[shift], shift, half, True)
    if give:
        put_cots(grad_ref, 8 * cells, total.astype(BF16))
    else:
        refs[0][...] = total


def finish_kernel(edge, part_ref, grad_ref, got_ref, out_ref, back_ref, rows_ref):
    half = edge // 2
    hh, cells, plane = half * half, half**3, edge * edge
    here = lax.axis_index("shard")
    got = jnp.concatenate(
        [got_ref[8 * cells : 9 * cells, :], got_ref[9 * cells : 10 * cells, :]], axis=1
    )
    rows_ref[...] = part_ref[...] + got.astype(F32)
    for i in range(half):
        for j in range(half):
            start = (i * half + j) * half
            out_ref[i, j] = rows_ref[start : start + half, :].astype(BF16)
    mine, theirs = grad_ref[...], got_ref[0 : 8 * cells, :]
    wide = jnp.concatenate(
        [jnp.where(here == 0, mine, theirs), jnp.where(here == 0, theirs, mine)], axis=1
    )
    blocks = 256 // plane
    order = plane_order(edge, blocks)
    for start in range(0, edge, blocks):
        pieces = []
        for b in range(blocks):
            first, i = (start + b) % 2, (start + b) // 2
            for inner in range(4):
                row = (4 * first + inner) * cells + i * hh
                pieces.append(wide[row : row + hh])
        back_ref[start * plane : (start + blocks) * plane, :] = dot(
            order, jnp.concatenate(pieces, axis=0), (0, 0)
        ).astype(BF16)


def place_kernel(parts, width, step, runs, has_base, *refs):
    out_ref, buffer, sem = refs[-3:]
    refs = refs[has_base:-3]
    place = lax.axis_index("dp")
    part = lax.rem(place, parts)
    copies = []
    for slot, (start, flip, pieces) in enumerate(runs):
        count = pieces[0][3]
        for index, offset, distance, _ in pieces:
            group = (part ^ distance) // 2
            rows = pl.ds(pl.multiple_of(group * width, width), width)
            buffer[start : start + count, rows, flip * LANES : (flip + 1) * LANES] = refs[index][
                offset : offset + count
            ].astype(F32)
        side = lax.rem(place, 2) ^ flip
        cols = pl.ds(pl.multiple_of(side * LANES, LANES), LANES)
        copy = pltpu.make_async_copy(
            buffer.at[start : start + count, :, flip * LANES : (flip + 1) * LANES],
            out_ref.at[start : start + count, :, cols],
            sem.at[slot],
        )
        copy.start()
        copies.append(copy)
    for copy in copies:
        copy.wait()


def vmem_call(body, outs, flops=0, scratch=(), **kwargs):
    space = pl.BlockSpec(memory_space=pltpu.VMEM)
    return pl.pallas_call(
        body,
        out_shape=outs,
        out_specs=jax.tree.map(lambda _: space, outs),
        scratch_shapes=scratch,
        compiler_params=pltpu.CompilerParams(vmem_limit_bytes=VMEM_BYTES),
        cost_estimate=pl.CostEstimate(flops=flops, bytes_accessed=1 << 20, transcendentals=0),
        **kwargs,
    )


def shape(dims, dtype=BF16):
    return jax.ShapeDtypeStruct(dims, dtype)


def after(value, *others):
    return lax.optimization_barrier((value, *others))[0]


def shards(groups_of, shards_of, inputs, cotangent, weights):
    edge, chans = inputs.shape[1], inputs.shape[4]
    half = edge // 2
    cells = half**3
    count, own_chans = weights.shape[0], weights.shape[1]
    parts = PARTS
    groups = parts // 2
    width = LANES // groups
    values = inputs.reshape(edge**3, chans)
    rows = cotangent.reshape(cotangent.shape[1:])
    row_buffer = [pltpu.VMEM((cells, chans), F32)]

    def across(value, distance):
        return lax.ppermute(value, "dp", [(i, i ^ distance) for i in range(groups_of)])

    def swap(value):
        return lax.ppermute(value, "shard", [(0, 1), (1, 0)])

    def deliver(value, distance):
        pairs = []
        for i in range(groups_of):
            for j in range(shards_of):
                pairs.append((i * shards_of + j, (i ^ (2 * distance)) * shards_of + (j ^ (i % 2))))
        return lax.ppermute(value, ("dp", "shard"), pairs)

    values2, rows2 = across(values, 1), across(rows, 1)
    send, own = vmem_call(
        functools.partial(sort_kernel, edge),
        (shape((10 * cells, LANES)),) * 2,
        scratch=row_buffer
        + [
            pltpu.VMEM(values.shape, BF16),
            pltpu.VMEM(rows.shape, BF16),
            pltpu.SemaphoreType.DMA((2,)),
        ],
        in_specs=[pl.BlockSpec(memory_space=pl.ANY)] * 2,
    )(values, rows)
    pieces = vmem_call(
        functools.partial(pack_kernel, edge, groups),
        (shape((8 * cells, LANES)),) * groups,
        scratch=row_buffer,
    )(own, send, values2, rows2)
    splits = SPLITS
    got = [deliver(pieces[distance], distance) for distance in DELIVERY]
    if SWAP == 1:
        send = after(send, *pieces)
    elif SWAP == 2:
        send = after(send, *got)
    other = swap(send)

    part, grad = vmem_call(
        functools.partial(sample_kernel, half, False),
        (shape((cells, chans), F32), shape((8 * cells, LANES))),
    )(own, weights)
    if SAMPLE == 0:
        other, part, grad = lax.optimization_barrier((other, part, grad))
    (back,) = vmem_call(
        functools.partial(sample_kernel, half, True), (shape((10 * cells, LANES)),)
    )(other, weights)
    if SAMPLE == 0:
        *got, back = lax.optimization_barrier((*got, back))
    elif SAMPLE == 1:
        *got, part, grad = lax.optimization_barrier((*got, part, grad))
    totals, sums = {}, []
    for turn, index in enumerate(ORDER):
        n, start = splits[index], sum(splits[:index])
        operands = got
        if turn == 1 and STAGGER:
            operands = lax.optimization_barrier((*got, totals[ORDER[0]]))[:-1]
        keep, give = vmem_call(
            functools.partial(weight_kernel, half, groups, start, n),
            (shape((n, width, LANES), F32), shape((n, width, LANES))),
        )(*operands)
        sums.append(give)
        if turn == 0 and BACK == 3:
            back = after(back, give)
        totals[index] = (keep + across(give, 1).astype(F32)).astype(BF16)
        if turn == 0 and BACK == 4:
            back = after(back, totals[index])
    if BACK == 1:
        back = after(back, *totals.values())
    elif BACK == 2:
        back = after(back, *sums)
    returned = swap(back)
    outputs, input_grad = vmem_call(
        functools.partial(finish_kernel, edge),
        (shape(rows.shape), shape((edge**3, chans))),
        scratch=row_buffer,
    )(part, grad, returned)

    held = []
    for turn, index in enumerate(ORDER):
        total = totals[index]
        if turn == 1 and DELAY == 1:
            total = after(total, other)
        if turn == 1 and DELAY == 2:
            total = after(total, back)
        distance = parts
        while distance < groups_of:
            arrived = across(total, distance)
            if turn == FINISH:
                arrived, outputs, input_grad = lax.optimization_barrier((arrived, outputs, input_grad))
            total = (total.astype(F32) + arrived.astype(F32)).astype(BF16)
            distance *= 2
        held.append(total)
    direct, crossed = [None] * len(splits), [None] * len(splits)
    for index, total in zip(ORDER, held):
        direct[index] = [total] + [across(total, distance) for distance in GATHER]
    for index in ORDER:
        crossed[index] = across(jnp.concatenate(direct[index], axis=0), 1)
    base = None

    def put(base, operands, runs):
        have = [] if base is None else [base]
        return pl.pallas_call(
            functools.partial(place_kernel, parts, width, BLOCK, runs, len(have)),
            in_specs=[pl.BlockSpec(memory_space=pl.ANY)] * len(have)
            + [pl.BlockSpec(memory_space=pltpu.VMEM)] * len(operands),
            out_specs=pl.BlockSpec(memory_space=pl.ANY),
            out_shape=shape((count, own_chans, chans), F32),
            scratch_shapes=[
                pltpu.VMEM((count, own_chans, chans), F32),
                pltpu.SemaphoreType.DMA((len(runs),)),
            ],
            input_output_aliases={0: 0} if have else {},
            compiler_params=pltpu.CompilerParams(vmem_limit_bytes=VMEM_BYTES),
        )(*have, *operands)

    def runs_of(indices, sets):
        runs, at = [], 0
        for index, kinds in zip(indices, sets):
            n, first = splits[index], sum(splits[:index])
            for kind in kinds:
                for low in range(0, n, BLOCK):
                    size = min(BLOCK, n - low)
                    pieces = []
                    for order, distance in enumerate((0,) + GATHER):
                        if kind == 0:
                            pieces.append((at + order, low, distance, size))
                        else:
                            pieces.append((at, order * n + low, distance, size))
                    runs.append((first + low, kind, pieces))
                at += 1 if kind else 1 + len(GATHER)
        return runs

    if PLACE == 0:
        base = put(None, sum(direct, []), runs_of(range(len(splits)), [(0,)] * len(splits)))
        base = put(base, crossed, runs_of(range(len(splits)), [(1,)] * len(splits)))
    else:
        early, late = ORDER[0], ORDER[1]
        base = put(None, direct[early] + [crossed[early]], runs_of([early], [(0, 1)]))
        if PLACE == 2:
            *there, base = lax.optimization_barrier((*direct[late], base))
            direct[late] = list(there)
            crossed[late] = across(jnp.concatenate(there, axis=0), 1)
        base = put(base, direct[late], runs_of([late], [(0,)]))
        base = put(base, [crossed[late]], runs_of([late], [(1,)]))
    return outputs.reshape(cotangent.shape), input_grad.reshape(inputs.shape), base


def build_cols(values):
    edge = values.shape[0]
    half = edge // 2
    width = values.shape[3]
    act = jax.nn.silu(values.astype(jnp.float32)).astype(jnp.bfloat16)
    padded = jnp.pad(act, ((1, 1), (1, 1), (1, 1), (0, 0)))
    pieces = []
    for first in range(3):
        for second in range(3):
            for third in range(3):
                pieces.append(
                    padded[
                        first : first + edge : 2,
                        second : second + edge : 2,
                        third : third + edge : 2,
                    ]
                )
    pieces.append(values[0::2, 0::2, 0::2])
    return jnp.stack(pieces, axis=3).reshape(half * half * half, 28, width)


def spread_back(values, grad_rows, piece, half):
    width = piece.shape[1]
    edge = 2 * half
    grid = jnp.zeros((edge + 2, edge + 2, edge + 2, width), jnp.float32)
    for first in range(3):
        block = jnp.einsum(
            "qo,tco->qtc",
            grad_rows,
            piece[9 * first : 9 * first + 9],
            preferred_element_type=jnp.float32,
        )
        block = block.reshape(half, half, half, 9, width)
        for second in range(3):
            for third in range(3):
                grid = grid.at[
                    first : first + edge : 2, second : second + edge : 2, third : third + edge : 2
                ].add(block[:, :, :, 3 * second + third])
    direct = jnp.einsum(
        "qo,co->qc", grad_rows, piece[27], preferred_element_type=jnp.float32
    ).reshape(half, half, half, width)
    own = values.astype(jnp.float32)
    sigma = jax.nn.sigmoid(own)
    grad_in = grid[1:-1, 1:-1, 1:-1] * sigma * (1.0 + own * (1.0 - sigma))
    grad_in = grad_in.at[0::2, 0::2, 0::2].add(direct)
    return grad_in.astype(jnp.bfloat16)


def general(inputs, cotangent, weights):
    values = inputs[0]
    edge = values.shape[0]
    half = edge // 2
    chans = values.shape[3]
    cols = build_cols(values)
    grad_rows = cotangent[0].reshape(half * half * half, chans)
    result = jnp.einsum(
        "qtc,tco->qo",
        cols,
        lax.all_gather(weights, "shard", axis=1, tiled=True),
        preferred_element_type=jnp.float32,
    )
    grad_in = spread_back(
        values, grad_rows, lax.all_gather(weights, "shard", axis=1, tiled=True), half
    )
    group_values = lax.all_to_all(inputs, "shard", split_axis=4, concat_axis=0, tiled=True)
    group_grads = lax.all_gather(cotangent, "shard", axis=0, tiled=True)
    count = group_values.shape[0]
    group_cols = jax.vmap(build_cols)(group_values)
    group_rows = group_grads.reshape(count, half * half * half, chans)
    per_sample = jnp.einsum(
        "sqtc,sqo->stco", group_cols, group_rows, preferred_element_type=jnp.float32
    )
    owned = jnp.sum(per_sample.astype(jnp.bfloat16).astype(jnp.float32), axis=0)
    weight_grad = lax.psum(owned, "dp")
    outputs = result.astype(jnp.bfloat16).reshape(1, half, half, half, chans)
    return (outputs, grad_in.reshape(1, edge, edge, edge, chans), weight_grad)


def fits(mesh, inputs, cotangent, weights):
    groups_of, shards_of = mesh.shape["dp"], mesh.shape["shard"]
    edge, chans = inputs.shape[1], inputs.shape[4]
    ratio = groups_of // PARTS
    return (
        shards_of == 2
        and chans == shards_of * LANES
        and inputs.shape[0] == groups_of * shards_of
        and inputs.shape[1:4] == (8, 8, 8)
        and groups_of % PARTS == 0
        and ratio & (ratio - 1) == 0
    )


def solution(mesh):
    rows = P(("dp", "shard"), None, None, None, None)
    kernel = P(None, "shard", None)

    def whole(inputs, cotangent, weights):
        body = general
        if fits(mesh, inputs, cotangent, weights):
            body = functools.partial(shards, mesh.shape["dp"], mesh.shape["shard"])
        return jax.shard_map(
            body,
            mesh=mesh,
            in_specs=(rows, rows, kernel),
            out_specs=(rows, rows, kernel),
            check_vma=False,
        )(inputs, cotangent, weights)

    return whole
```

```python
import functools

import jax
import jax.numpy as jnp
from jax import lax
from jax.experimental import pallas as pl
from jax.experimental.pallas import tpu as pltpu
from jax.sharding import PartitionSpec as P

LANES = 128
PARTS = 8
DELIVERY = (3, 1, 2, 0)
GATHER = (2, 4, 6)
SPLITS = (14, 14)
BLOCK = 7
ORDER = (0, 1)
SWAP = 2
SAMPLE = 1
STAGGER = True
BACK = 4
FINISH = 1
DELAY = 0
PLACE = 3
RELAY = False
LATE_OTHER = 9
VMEM_BYTES = 48 * 1024 * 1024
BF16 = jnp.bfloat16
F32 = jnp.float32

TAP_CLASS = (1, 0, 1)
TAP_SHIFT = (1, 0, 0)


def tap_table():
    table = []
    for first in range(3):
        for second in range(3):
            for third in range(3):
                taps = (first, second, third)
                table.append(
                    (tuple(TAP_CLASS[t] for t in taps), tuple(TAP_SHIFT[t] for t in taps))
                )
    return table


def class_index(parity):
    return 4 * parity[0] + 2 * parity[1] + parity[2]


def dot(left, right, contract=(1, 0)):
    return lax.dot_general(
        left, right, (((contract[0],), (contract[1],)), ((), ())), preferred_element_type=F32
    )


def row_digits(rows, half):
    row = lax.broadcasted_iota(jnp.int32, (rows, 1), 0)
    return (row // (half * half)) % half, (row // half) % half, row % half


def shift_rows(value, shift, half, forward):
    if not any(shift):
        return value
    rows = value.shape[0]
    offset = (shift[0] * half + shift[1]) * half + shift[2]
    keep = None
    for digit, step in zip(row_digits(rows, half), shift):
        if step:
            inside = digit >= step if forward else digit < half - step
            keep = inside if keep is None else keep & inside
    moved = pltpu.roll(value, offset if forward else rows - offset, 0)
    return jnp.where(keep, moved, 0.0)


def plane_order(edge, blocks):
    half = edge // 2
    plane = edge * edge
    size = blocks * plane
    row = lax.broadcasted_iota(jnp.int32, (size, size), 0)
    col = lax.broadcasted_iota(jnp.int32, (size, size), 1)
    inner = row % plane
    parity, cell = inner // (half * half), inner % (half * half)
    second = 2 * (cell // half) + parity // 2
    third = 2 * (cell % half) + parity % 2
    return (col == (row // plane) * plane + second * edge + third).astype(BF16)


def rows_in(rows_ref, cot_ref, half):
    for i in range(half):
        for j in range(half):
            start = (i * half + j) * half
            rows_ref[start : start + half, :] = cot_ref[i, j].astype(F32)
    return rows_ref[...].astype(BF16)


def sorted_cells(edge, ref):
    half = edge // 2
    hh, plane = half * half, edge * edge
    blocks = 256 // plane
    order = plane_order(edge, blocks)
    planes = []
    for start in range(0, edge, blocks):
        moved = dot(order, ref[start * plane : (start + blocks) * plane, :]).astype(BF16)
        planes += [moved[b * plane : (b + 1) * plane] for b in range(blocks)]
    return [
        jnp.concatenate([planes[2 * i + first][inner * hh : (inner + 1) * hh] for i in range(half)], axis=0)
        for first in range(2)
        for inner in range(4)
    ]


def put_cots(ref, start, cots):
    cells = cots.shape[0]
    for side in range(2):
        ref[start + side * cells : start + (side + 1) * cells, :] = cots[:, side * LANES : (side + 1) * LANES]


def sort_kernel(edge, x_hbm, cot_hbm, send_ref, own_ref, rows_ref, x_ref, cot_ref, sems):
    half = edge // 2
    cells = half**3
    here = lax.axis_index("shard")
    copies = [
        pltpu.make_async_copy(x_hbm, x_ref, sems.at[0]),
        pltpu.make_async_copy(cot_hbm, cot_ref, sems.at[1]),
    ]
    for copy in copies:
        copy.start()
    for copy in copies:
        copy.wait()
    for index, value in enumerate(sorted_cells(edge, x_ref)):
        low, high = value[:, :LANES], value[:, LANES:]
        own_ref[index * cells : (index + 1) * cells, :] = jnp.where(here == 0, low, high)
        send_ref[index * cells : (index + 1) * cells, :] = jnp.where(here == 0, high, low)
    cots = rows_in(rows_ref, cot_ref, half)
    put_cots(own_ref, 8 * cells, cots)
    put_cots(send_ref, 8 * cells, cots)


def pack_kernel(edge, groups, own_ref, send_ref, x2_ref, cot2_ref, *refs):
    piece_refs, rows_ref = refs[:groups], refs[groups]
    half = edge // 2
    cells = half**3
    width = LANES // groups
    place = lax.axis_index("dp")
    core, group = lax.rem(place, 2), lax.rem(place // 2, groups)
    target = lax.axis_index("shard") ^ core
    samples = [
        [
            jnp.where(core == 0, own_ref[rows, :], send_ref[rows, :])
            for rows in (slice(index * cells, (index + 1) * cells) for index in range(8))
        ],
        [
            jnp.where(target == 0, value[:, :LANES], value[:, LANES:])
            for value in sorted_cells(edge, x2_ref)
        ],
    ]
    size = 4 * LANES
    row = lax.broadcasted_iota(jnp.int32, (size, size), 0)
    col = lax.broadcasted_iota(jnp.int32, (size, size), 1)
    source = ((col // width) % 4) * LANES + (col // LANES) * width + col % width
    lane_order = (row == source).astype(BF16)
    wide = jnp.concatenate(
        [
            jnp.concatenate(classes[4 * first : 4 * first + 4], axis=1)
            for classes in samples
            for first in range(2)
        ],
        axis=0,
    )
    packed = dot(wide, lane_order).astype(BF16)
    cots = rows_in(rows_ref, cot2_ref, half)
    for distance, ref in enumerate(piece_refs):
        owner = group ^ distance
        value = packed[:, (groups - 1) * LANES :]
        for index in range(groups - 1):
            value = jnp.where(owner == index, packed[:, index * LANES : (index + 1) * LANES], value)
        ref[0 : 4 * cells, :] = value
        ref[4 * cells : 6 * cells, :] = own_ref[8 * cells : 10 * cells, :]
        put_cots(ref, 6 * cells, cots)


def weight_kernel(half, groups, start, count, *refs):
    got_refs, (keep_ref, give_ref) = refs[:groups], refs[groups:]
    cells = half**3
    width = LANES // groups
    chans = 2 * LANES
    core = lax.rem(lax.axis_index("dp"), 2)
    table = tap_table()
    wanted = range(start, start + count)
    needs = {(table[tap][0][0], table[tap][1][0]) for tap in wanted if tap < len(table)}

    def gather(offset):
        return jnp.concatenate(
            [ref[start : start + cells, :] for ref in got_refs for start in offset], axis=0
        )

    raw, acts = {}, {}
    for first in range(2):
        raw[first] = gather([first * cells, (2 + first) * cells])
        wide = raw[first].astype(F32)
        acts[first] = (wide / (1.0 + jnp.exp(-wide))).astype(BF16)
    cots = jnp.concatenate(
        [gather([(4 + side) * cells, (6 + side) * cells]) for side in range(2)], axis=1
    )
    sums = {}
    for si in range(2):
        firsts = [first for first in range(2) if (first, si) in needs]
        if firsts:
            right = jnp.concatenate(
                [
                    shift_rows(cots.astype(F32), (si, sj, sk), half, False).astype(BF16)
                    for sj in range(2)
                    for sk in range(2)
                ],
                axis=1,
            )
            for first in firsts:
                sums[first, si] = dot(acts[first], right, (0, 0))
    for tap in wanted:
        if tap < len(table):
            parity, shift = table[tap]
            row = (2 * parity[1] + parity[2]) * width
            col = (2 * shift[1] + shift[2]) * chans
            value = sums[parity[0], shift[0]][row : row + width, col : col + chans]
        else:
            value = dot(raw[0], cots, (0, 0))[:width]
        low, high = value[:, :LANES], value[:, LANES:]
        keep_ref[tap - start] = jnp.where(core == 0, low, high)
        give_ref[tap - start] = jnp.where(core == 0, high, low).astype(BF16)


def sample_kernel(half, give, own_ref, w_ref, *refs):
    grad_ref = refs[-1]
    cells = half**3
    count = len(tap_table())
    cots = jnp.concatenate([own_ref[(8 + side) * cells : (9 + side) * cells, :] for side in range(2)], axis=1).astype(F32)
    moved, gathered = {}, {}
    shifts = [(si, sj, sk) for si in range(2) for sj in range(2) for sk in range(2)]
    for shift in shifts:
        moved[shift] = shift_rows(cots, shift, half, False).astype(BF16)
    for index in range(8):
        rows = slice(index * cells, (index + 1) * cells)
        value = own_ref[rows, :]
        wide = value.astype(F32)
        sigma = 1.0 / (1.0 + jnp.exp(-wide))
        act = (wide * sigma).astype(BF16)
        back = None
        for tap, (parity, shift) in enumerate(tap_table()):
            if class_index(parity) != index:
                continue
            weight = w_ref[tap]
            term = dot(act, weight)
            gathered[shift] = term if shift not in gathered else gathered[shift] + term
            term = dot(moved[shift], weight, (1, 1))
            back = term if back is None else back + term
        grad = back * sigma * (1.0 + wide * (1.0 - sigma))
        if index == 0:
            weight = w_ref[count]
            gathered[0, 0, 0] = gathered[0, 0, 0] + dot(value, weight)
            grad = grad + dot(moved[0, 0, 0], weight, (1, 1))
        grad_ref[rows, :] = grad.astype(BF16)
    total = gathered[0, 0, 0]
    for shift in shifts[1:]:
        total = total + shift_rows(gathered[shift], shift, half, True)
    if give:
        put_cots(grad_ref, 8 * cells, total.astype(BF16))
    else:
        refs[0][...] = total


def finish_kernel(edge, part_ref, grad_ref, got_ref, out_ref, back_ref, rows_ref):
    half = edge // 2
    hh, cells, plane = half * half, half**3, edge * edge
    here = lax.axis_index("shard")
    got = jnp.concatenate(
        [got_ref[8 * cells : 9 * cells, :], got_ref[9 * cells : 10 * cells, :]], axis=1
    )
    rows_ref[...] = part_ref[...] + got.astype(F32)
    for i in range(half):
        for j in range(half):
            start = (i * half + j) * half
            out_ref[i, j] = rows_ref[start : start + half, :].astype(BF16)
    mine, theirs = grad_ref[...], got_ref[0 : 8 * cells, :]
    wide = jnp.concatenate(
        [jnp.where(here == 0, mine, theirs), jnp.where(here == 0, theirs, mine)], axis=1
    )
    blocks = 256 // plane
    order = plane_order(edge, blocks)
    for start in range(0, edge, blocks):
        pieces = []
        for b in range(blocks):
            first, i = (start + b) % 2, (start + b) // 2
            for inner in range(4):
                row = (4 * first + inner) * cells + i * hh
                pieces.append(wide[row : row + hh])
        back_ref[start * plane : (start + blocks) * plane, :] = dot(
            order, jnp.concatenate(pieces, axis=0), (0, 0)
        ).astype(BF16)


def place_kernel(parts, width, step, runs, has_base, *refs):
    out_ref, buffer, sem = refs[-3:]
    refs = refs[has_base:-3]
    place = lax.axis_index("dp")
    part = lax.rem(place, parts)
    copies = []
    for slot, (start, flip, pieces) in enumerate(runs):
        count = pieces[0][3]
        for index, offset, distance, _ in pieces:
            group = (part ^ distance) // 2
            rows = pl.ds(pl.multiple_of(group * width, width), width)
            buffer[start : start + count, rows, flip * LANES : (flip + 1) * LANES] = refs[index][
                offset : offset + count
            ].astype(F32)
        side = lax.rem(place, 2) ^ flip
        cols = pl.ds(pl.multiple_of(side * LANES, LANES), LANES)
        copy = pltpu.make_async_copy(
            buffer.at[start : start + count, :, flip * LANES : (flip + 1) * LANES],
            out_ref.at[start : start + count, :, cols],
            sem.at[slot],
        )
        copy.start()
        copies.append(copy)
    for copy in copies:
        copy.wait()


def vmem_call(body, outs, flops=0, scratch=(), **kwargs):
    space = pl.BlockSpec(memory_space=pltpu.VMEM)
    return pl.pallas_call(
        body,
        out_shape=outs,
        out_specs=jax.tree.map(lambda _: space, outs),
        scratch_shapes=scratch,
        compiler_params=pltpu.CompilerParams(vmem_limit_bytes=VMEM_BYTES),
        cost_estimate=pl.CostEstimate(flops=flops, bytes_accessed=1 << 20, transcendentals=0),
        **kwargs,
    )


def shape(dims, dtype=BF16):
    return jax.ShapeDtypeStruct(dims, dtype)


def after(value, *others):
    return lax.optimization_barrier((value, *others))[0]


def shards(groups_of, shards_of, inputs, cotangent, weights):
    edge, chans = inputs.shape[1], inputs.shape[4]
    half = edge // 2
    cells = half**3
    count, own_chans = weights.shape[0], weights.shape[1]
    parts = PARTS
    groups = parts // 2
    width = LANES // groups
    values = inputs.reshape(edge**3, chans)
    rows = cotangent.reshape(cotangent.shape[1:])
    row_buffer = [pltpu.VMEM((cells, chans), F32)]

    def across(value, distance):
        return lax.ppermute(value, "dp", [(i, i ^ distance) for i in range(groups_of)])

    def swap(value):
        return lax.ppermute(value, "shard", [(0, 1), (1, 0)])

    def deliver(value, distance):
        pairs = []
        for i in range(groups_of):
            for j in range(shards_of):
                pairs.append((i * shards_of + j, (i ^ (2 * distance)) * shards_of + (j ^ (i % 2))))
        return lax.ppermute(value, ("dp", "shard"), pairs)

    values2, rows2 = across(values, 1), across(rows, 1)
    send, own = vmem_call(
        functools.partial(sort_kernel, edge),
        (shape((10 * cells, LANES)),) * 2,
        scratch=row_buffer
        + [
            pltpu.VMEM(values.shape, BF16),
            pltpu.VMEM(rows.shape, BF16),
            pltpu.SemaphoreType.DMA((2,)),
        ],
        in_specs=[pl.BlockSpec(memory_space=pl.ANY)] * 2,
    )(values, rows)
    pieces = vmem_call(
        functools.partial(pack_kernel, edge, groups),
        (shape((8 * cells, LANES)),) * groups,
        scratch=row_buffer,
    )(own, send, values2, rows2)
    splits = SPLITS
    got = [deliver(pieces[distance], distance) for distance in DELIVERY]
    if SWAP == 1:
        send = after(send, *pieces)
    elif SWAP == 2:
        send = after(send, *got)
    other = swap(send)

    if LATE_OTHER == 0:
        other, got[0] = lax.optimization_barrier((other, got[0]))
    part, grad = vmem_call(
        functools.partial(sample_kernel, half, False),
        (shape((cells, chans), F32), shape((8 * cells, LANES))),
    )(own, weights)
    if SAMPLE == 0:
        other, part, grad = lax.optimization_barrier((other, part, grad))
    (back,) = vmem_call(
        functools.partial(sample_kernel, half, True), (shape((10 * cells, LANES)),)
    )(other, weights)
    if SAMPLE == 0:
        *got, back = lax.optimization_barrier((*got, back))
    elif SAMPLE == 1:
        *got, part, grad = lax.optimization_barrier((*got, part, grad))
    totals, sums = {}, []
    for turn, index in enumerate(ORDER):
        n, start = splits[index], sum(splits[:index])
        operands = got
        if turn == 1 and STAGGER:
            operands = lax.optimization_barrier((*got, totals[ORDER[0]]))[:-1]
        keep, give = vmem_call(
            functools.partial(weight_kernel, half, groups, start, n),
            (shape((n, width, LANES), F32), shape((n, width, LANES))),
        )(*operands)
        sums.append(give)
        if turn == 0 and BACK == 3:
            back = after(back, give)
        totals[index] = (keep + across(give, 1).astype(F32)).astype(BF16)
        if turn == 0 and BACK == 4:
            back = after(back, totals[index])
    if BACK == 1:
        back = after(back, *totals.values())
    elif BACK == 2:
        back = after(back, *sums)
    returned = swap(back)
    outputs, input_grad = vmem_call(
        functools.partial(finish_kernel, edge),
        (shape(rows.shape), shape((edge**3, chans))),
        scratch=row_buffer,
    )(part, grad, returned)

    held = []
    for turn, index in enumerate(ORDER):
        total = totals[index]
        if turn == 1 and DELAY == 1:
            total = after(total, other)
        if turn == 1 and DELAY == 2:
            total = after(total, back)
        distance = parts
        while distance < groups_of:
            arrived = across(total, distance)
            if turn == FINISH:
                arrived, outputs, input_grad = lax.optimization_barrier((arrived, outputs, input_grad))
            total = (total.astype(F32) + arrived.astype(F32)).astype(BF16)
            distance *= 2
        held.append(total)
    direct, crossed = [None] * len(splits), [None] * len(splits)
    for index, total in zip(ORDER, held):
        if RELAY and index == ORDER[0]:
            behind, beside = across(total, 4), across(total, 2)
            found = {4: behind, 2: beside, 6: across(behind, 2)}
            direct[index] = [total] + [found[distance] for distance in GATHER]
        else:
            direct[index] = [total] + [across(total, distance) for distance in GATHER]
    for index in ORDER:
        crossed[index] = across(jnp.concatenate(direct[index], axis=0), 1)
    base = None

    def put(base, operands, runs):
        have = [] if base is None else [base]
        return pl.pallas_call(
            functools.partial(place_kernel, parts, width, BLOCK, runs, len(have)),
            in_specs=[pl.BlockSpec(memory_space=pl.ANY)] * len(have)
            + [pl.BlockSpec(memory_space=pltpu.VMEM)] * len(operands),
            out_specs=pl.BlockSpec(memory_space=pl.ANY),
            out_shape=shape((count, own_chans, chans), F32),
            scratch_shapes=[
                pltpu.VMEM((count, own_chans, chans), F32),
                pltpu.SemaphoreType.DMA((len(runs),)),
            ],
            input_output_aliases={0: 0} if have else {},
            compiler_params=pltpu.CompilerParams(vmem_limit_bytes=VMEM_BYTES),
        )(*have, *operands)

    def runs_of(indices, sets):
        runs, at = [], 0
        for index, kinds in zip(indices, sets):
            n, first = splits[index], sum(splits[:index])
            for kind in kinds:
                for low in range(0, n, BLOCK):
                    size = min(BLOCK, n - low)
                    pieces = []
                    for order, distance in enumerate((0,) + GATHER):
                        if kind == 0:
                            pieces.append((at + order, low, distance, size))
                        else:
                            pieces.append((at, order * n + low, distance, size))
                    runs.append((first + low, kind, pieces))
                at += 1 if kind else 1 + len(GATHER)
        return runs

    if PLACE == 3:
        early, late = ORDER[0], ORDER[1]
        base = put(None, direct[early] + [crossed[early]] + direct[late], runs_of([early, late], [(0, 1), (0,)]))
        base = put(base, [crossed[late]], runs_of([late], [(1,)]))
    elif PLACE == 0:
        base = put(None, sum(direct, []), runs_of(range(len(splits)), [(0,)] * len(splits)))
        base = put(base, crossed, runs_of(range(len(splits)), [(1,)] * len(splits)))
    else:
        early, late = ORDER[0], ORDER[1]
        base = put(None, direct[early] + [crossed[early]], runs_of([early], [(0, 1)]))
        if PLACE == 2:
            *there, base = lax.optimization_barrier((*direct[late], base))
            direct[late] = list(there)
            crossed[late] = across(jnp.concatenate(there, axis=0), 1)
        base = put(base, direct[late], runs_of([late], [(0,)]))
        base = put(base, [crossed[late]], runs_of([late], [(1,)]))
    return outputs.reshape(cotangent.shape), input_grad.reshape(inputs.shape), base


def build_cols(values):
    edge = values.shape[0]
    half = edge // 2
    width = values.shape[3]
    act = jax.nn.silu(values.astype(jnp.float32)).astype(jnp.bfloat16)
    padded = jnp.pad(act, ((1, 1), (1, 1), (1, 1), (0, 0)))
    pieces = []
    for first in range(3):
        for second in range(3):
            for third in range(3):
                pieces.append(
                    padded[
                        first : first + edge : 2,
                        second : second + edge : 2,
                        third : third + edge : 2,
                    ]
                )
    pieces.append(values[0::2, 0::2, 0::2])
    return jnp.stack(pieces, axis=3).reshape(half * half * half, 28, width)


def spread_back(values, grad_rows, piece, half):
    width = piece.shape[1]
    edge = 2 * half
    grid = jnp.zeros((edge + 2, edge + 2, edge + 2, width), jnp.float32)
    for first in range(3):
        block = jnp.einsum(
            "qo,tco->qtc",
            grad_rows,
            piece[9 * first : 9 * first + 9],
            preferred_element_type=jnp.float32,
        )
        block = block.reshape(half, half, half, 9, width)
        for second in range(3):
            for third in range(3):
                grid = grid.at[
                    first : first + edge : 2, second : second + edge : 2, third : third + edge : 2
                ].add(block[:, :, :, 3 * second + third])
    direct = jnp.einsum(
        "qo,co->qc", grad_rows, piece[27], preferred_element_type=jnp.float32
    ).reshape(half, half, half, width)
    own = values.astype(jnp.float32)
    sigma = jax.nn.sigmoid(own)
    grad_in = grid[1:-1, 1:-1, 1:-1] * sigma * (1.0 + own * (1.0 - sigma))
    grad_in = grad_in.at[0::2, 0::2, 0::2].add(direct)
    return grad_in.astype(jnp.bfloat16)


def general(inputs, cotangent, weights):
    values = inputs[0]
    edge = values.shape[0]
    half = edge // 2
    chans = values.shape[3]
    cols = build_cols(values)
    grad_rows = cotangent[0].reshape(half * half * half, chans)
    result = jnp.einsum(
        "qtc,tco->qo",
        cols,
        lax.all_gather(weights, "shard", axis=1, tiled=True),
        preferred_element_type=jnp.float32,
    )
    grad_in = spread_back(
        values, grad_rows, lax.all_gather(weights, "shard", axis=1, tiled=True), half
    )
    group_values = lax.all_to_all(inputs, "shard", split_axis=4, concat_axis=0, tiled=True)
    group_grads = lax.all_gather(cotangent, "shard", axis=0, tiled=True)
    count = group_values.shape[0]
    group_cols = jax.vmap(build_cols)(group_values)
    group_rows = group_grads.reshape(count, half * half * half, chans)
    per_sample = jnp.einsum(
        "sqtc,sqo->stco", group_cols, group_rows, preferred_element_type=jnp.float32
    )
    owned = jnp.sum(per_sample.astype(jnp.bfloat16).astype(jnp.float32), axis=0)
    weight_grad = lax.psum(owned, "dp")
    outputs = result.astype(jnp.bfloat16).reshape(1, half, half, half, chans)
    return (outputs, grad_in.reshape(1, edge, edge, edge, chans), weight_grad)


def fits(mesh, inputs, cotangent, weights):
    groups_of, shards_of = mesh.shape["dp"], mesh.shape["shard"]
    edge, chans = inputs.shape[1], inputs.shape[4]
    ratio = groups_of // PARTS
    return (
        shards_of == 2
        and chans == shards_of * LANES
        and inputs.shape[0] == groups_of * shards_of
        and inputs.shape[1:4] == (8, 8, 8)
        and groups_of % PARTS == 0
        and ratio & (ratio - 1) == 0
    )


def solution(mesh):
    rows = P(("dp", "shard"), None, None, None, None)
    kernel = P(None, "shard", None)

    def whole(inputs, cotangent, weights):
        body = general
        if fits(mesh, inputs, cotangent, weights):
            body = functools.partial(shards, mesh.shape["dp"], mesh.shape["shard"])
        return jax.shard_map(
            body,
            mesh=mesh,
            in_specs=(rows, rows, kernel),
            out_specs=(rows, rows, kernel),
            check_vma=False,
        )(inputs, cotangent, weights)

    return whole
```

```python
import functools

import jax
import jax.numpy as jnp
from jax import lax
from jax.experimental import pallas as pl
from jax.experimental.pallas import tpu as pltpu
from jax.sharding import PartitionSpec as P

LANES = 128
PARTS = 8
DELIVERY = (1, 2, 3, 0)
GATHER = (2, 4, 6)
BLOCK = 7
VMEM_BYTES = 48 * 1024 * 1024
BF16 = jnp.bfloat16
F32 = jnp.float32

TAP_CLASS = (1, 0, 1)
TAP_SHIFT = (1, 0, 0)


def tap_table():
    table = []
    for first in range(3):
        for second in range(3):
            for third in range(3):
                taps = (first, second, third)
                table.append(
                    (tuple(TAP_CLASS[t] for t in taps), tuple(TAP_SHIFT[t] for t in taps))
                )
    return table


def class_index(parity):
    return 4 * parity[0] + 2 * parity[1] + parity[2]


def dot(left, right, contract=(1, 0)):
    return lax.dot_general(
        left, right, (((contract[0],), (contract[1],)), ((), ())), preferred_element_type=F32
    )


def row_digits(rows, half):
    row = lax.broadcasted_iota(jnp.int32, (rows, 1), 0)
    return (row // (half * half)) % half, (row // half) % half, row % half


def shift_rows(value, shift, half, forward):
    if not any(shift):
        return value
    rows = value.shape[0]
    offset = (shift[0] * half + shift[1]) * half + shift[2]
    keep = None
    for digit, step in zip(row_digits(rows, half), shift):
        if step:
            inside = digit >= step if forward else digit < half - step
            keep = inside if keep is None else keep & inside
    moved = pltpu.roll(value, offset if forward else rows - offset, 0)
    return jnp.where(keep, moved, 0.0)


def plane_order(edge, blocks):
    half = edge // 2
    plane = edge * edge
    size = blocks * plane
    row = lax.broadcasted_iota(jnp.int32, (size, size), 0)
    col = lax.broadcasted_iota(jnp.int32, (size, size), 1)
    inner = row % plane
    parity, cell = inner // (half * half), inner % (half * half)
    second = 2 * (cell // half) + parity // 2
    third = 2 * (cell % half) + parity % 2
    return (col == (row // plane) * plane + second * edge + third).astype(BF16)


def rows_in(rows_ref, cot_ref, half):
    for i in range(half):
        for j in range(half):
            start = (i * half + j) * half
            rows_ref[start : start + half, :] = cot_ref[i, j].astype(F32)
    return rows_ref[...].astype(BF16)


def sorted_cells(edge, ref):
    half = edge // 2
    hh, plane = half * half, edge * edge
    blocks = 256 // plane
    order = plane_order(edge, blocks)
    planes = []
    for start in range(0, edge, blocks):
        moved = dot(order, ref[start * plane : (start + blocks) * plane, :]).astype(BF16)
        planes += [moved[b * plane : (b + 1) * plane] for b in range(blocks)]
    return [
        jnp.concatenate([planes[2 * i + first][inner * hh : (inner + 1) * hh] for i in range(half)], axis=0)
        for first in range(2)
        for inner in range(4)
    ]


def put_cots(ref, start, cots):
    cells = cots.shape[0]
    for side in range(2):
        ref[start + side * cells : start + (side + 1) * cells, :] = cots[:, side * LANES : (side + 1) * LANES]


def sort_kernel(edge, x_ref, keep_ref, send_ref):
    cells = (edge // 2) ** 3
    here = lax.axis_index("shard")
    for index, value in enumerate(sorted_cells(edge, x_ref)):
        low, high = value[:, :LANES], value[:, LANES:]
        keep_ref[index * cells : (index + 1) * cells, :] = jnp.where(here == 0, low, high)
        send_ref[index * cells : (index + 1) * cells, :] = jnp.where(here == 0, high, low)


def crossing(core, distance):
    return core ^ (bin(distance).count("1") % 2)


def pack_kernel(edge, groups, keep_ref, give_ref, cot_ref, x2_ref, cot2_ref, *refs):
    piece_refs, (own_ref, send_ref, rows_ref) = refs[:groups], refs[groups:]
    half = edge // 2
    cells = half**3
    width = LANES // groups
    place = lax.axis_index("dp")
    core, group = lax.rem(place, 2), lax.rem(place // 2, groups)
    here = lax.axis_index("shard")
    second = sorted_cells(edge, x2_ref)
    size = 4 * LANES
    row = lax.broadcasted_iota(jnp.int32, (size, size), 0)
    col = lax.broadcasted_iota(jnp.int32, (size, size), 1)
    source = ((col // width) % 4) * LANES + (col // LANES) * width + col % width
    lane_order = (row == source).astype(BF16)
    packed = []
    for ref, owner in ((keep_ref, here), (give_ref, 1 - here)):
        samples = [
            [ref[index * cells : (index + 1) * cells, :] for index in range(8)],
            [jnp.where(owner == 0, value[:, :LANES], value[:, LANES:]) for value in second],
        ]
        wide = jnp.concatenate(
            [
                jnp.concatenate(classes[4 * first : 4 * first + 4], axis=1)
                for classes in samples
                for first in range(2)
            ],
            axis=0,
        )
        packed.append(dot(wide, lane_order).astype(BF16))
    cots = [rows_in(rows_ref, ref, half) for ref in (cot_ref, cot2_ref)]
    for distance, ref in enumerate(piece_refs):
        owner = group ^ distance
        chosen = jnp.where(crossing(core, distance) == 0, packed[0], packed[1])
        value = chosen[:, (groups - 1) * LANES :]
        for index in range(groups - 1):
            value = jnp.where(owner == index, chosen[:, index * LANES : (index + 1) * LANES], value)
        ref[0 : 4 * cells, :] = value
        put_cots(ref, 4 * cells, cots[0])
        put_cots(ref, 6 * cells, cots[1])
    for ref, half_ref in ((own_ref, keep_ref), (send_ref, give_ref)):
        ref[0 : 8 * cells, :] = half_ref[...]
        put_cots(ref, 8 * cells, cots[0])


def weight_kernel(half, groups, start, count, *refs):
    got_refs, (keep_ref, give_ref) = refs[:groups], refs[groups:]
    cells = half**3
    width = LANES // groups
    chans = 2 * LANES
    core = lax.rem(lax.axis_index("dp"), 2)
    table = tap_table()
    wanted = range(start, start + count)
    needs = {(table[tap][0][0], table[tap][1][0]) for tap in wanted if tap < len(table)}

    def gather(offset):
        return jnp.concatenate(
            [ref[start : start + cells, :] for ref in got_refs for start in offset], axis=0
        )

    raw, acts = {}, {}
    for first in range(2):
        raw[first] = gather([first * cells, (2 + first) * cells])
        wide = raw[first].astype(F32)
        acts[first] = (wide / (1.0 + jnp.exp(-wide))).astype(BF16)
    cots = jnp.concatenate(
        [gather([(4 + side) * cells, (6 + side) * cells]) for side in range(2)], axis=1
    )
    sums = {}
    for si in range(2):
        firsts = [first for first in range(2) if (first, si) in needs]
        if firsts:
            right = jnp.concatenate(
                [
                    shift_rows(cots.astype(F32), (si, sj, sk), half, False).astype(BF16)
                    for sj in range(2)
                    for sk in range(2)
                ],
                axis=1,
            )
            for first in firsts:
                sums[first, si] = dot(acts[first], right, (0, 0))
    for tap in wanted:
        if tap < len(table):
            parity, shift = table[tap]
            row = (2 * parity[1] + parity[2]) * width
            col = (2 * shift[1] + shift[2]) * chans
            value = sums[parity[0], shift[0]][row : row + width, col : col + chans]
        else:
            value = dot(raw[0], cots, (0, 0))[:width]
        low, high = value[:, :LANES], value[:, LANES:]
        keep_ref[tap - start] = jnp.where(core == 0, low, high)
        give_ref[tap - start] = jnp.where(core == 0, high, low).astype(BF16)


def sample_kernel(half, give, own_ref, w_ref, *refs):
    grad_ref = refs[-1]
    cells = half**3
    count = len(tap_table())
    cots = jnp.concatenate([own_ref[(8 + side) * cells : (9 + side) * cells, :] for side in range(2)], axis=1).astype(F32)
    moved, gathered = {}, {}
    shifts = [(si, sj, sk) for si in range(2) for sj in range(2) for sk in range(2)]
    for shift in shifts:
        moved[shift] = shift_rows(cots, shift, half, False).astype(BF16)
    for index in range(8):
        rows = slice(index * cells, (index + 1) * cells)
        value = own_ref[rows, :]
        wide = value.astype(F32)
        sigma = 1.0 / (1.0 + jnp.exp(-wide))
        act = (wide * sigma).astype(BF16)
        back = None
        for tap, (parity, shift) in enumerate(tap_table()):
            if class_index(parity) != index:
                continue
            weight = w_ref[tap]
            term = dot(act, weight)
            gathered[shift] = term if shift not in gathered else gathered[shift] + term
            term = dot(moved[shift], weight, (1, 1))
            back = term if back is None else back + term
        grad = back * sigma * (1.0 + wide * (1.0 - sigma))
        if index == 0:
            weight = w_ref[count]
            gathered[0, 0, 0] = gathered[0, 0, 0] + dot(value, weight)
            grad = grad + dot(moved[0, 0, 0], weight, (1, 1))
        grad_ref[rows, :] = grad.astype(BF16)
    total = gathered[0, 0, 0]
    for shift in shifts[1:]:
        total = total + shift_rows(gathered[shift], shift, half, True)
    if give:
        put_cots(grad_ref, 8 * cells, total.astype(BF16))
    else:
        refs[0][...] = total


def finish_kernel(edge, part_ref, grad_ref, got_ref, out_ref, back_ref, rows_ref):
    half = edge // 2
    hh, cells, plane = half * half, half**3, edge * edge
    here = lax.axis_index("shard")
    got = jnp.concatenate(
        [got_ref[8 * cells : 9 * cells, :], got_ref[9 * cells : 10 * cells, :]], axis=1
    )
    rows_ref[...] = part_ref[...] + got.astype(F32)
    for i in range(half):
        for j in range(half):
            start = (i * half + j) * half
            out_ref[i, j] = rows_ref[start : start + half, :].astype(BF16)
    mine, theirs = grad_ref[...], got_ref[0 : 8 * cells, :]
    wide = jnp.concatenate(
        [jnp.where(here == 0, mine, theirs), jnp.where(here == 0, theirs, mine)], axis=1
    )
    blocks = 256 // plane
    order = plane_order(edge, blocks)
    for start in range(0, edge, blocks):
        pieces = []
        for b in range(blocks):
            first, i = (start + b) % 2, (start + b) // 2
            for inner in range(4):
                row = (4 * first + inner) * cells + i * hh
                pieces.append(wide[row : row + hh])
        back_ref[start * plane : (start + blocks) * plane, :] = dot(
            order, jnp.concatenate(pieces, axis=0), (0, 0)
        ).astype(BF16)


def place_kernel(parts, width, runs, has_base, *refs):
    out_ref, buffer, sem = refs[-3:]
    refs = refs[has_base:-3]
    place = lax.axis_index("dp")
    part = lax.rem(place, parts)
    copies = []
    for slot, (start, flip, pieces) in enumerate(runs):
        count = pieces[0][3]
        for index, offset, distance, _ in pieces:
            group = (part ^ distance) // 2
            rows = pl.ds(pl.multiple_of(group * width, width), width)
            buffer[start : start + count, rows, flip * LANES : (flip + 1) * LANES] = refs[index][
                offset : offset + count
            ].astype(F32)
        side = lax.rem(place, 2) ^ flip
        cols = pl.ds(pl.multiple_of(side * LANES, LANES), LANES)
        copy = pltpu.make_async_copy(
            buffer.at[start : start + count, :, flip * LANES : (flip + 1) * LANES],
            out_ref.at[start : start + count, :, cols],
            sem.at[slot],
        )
        copy.start()
        copies.append(copy)
    for copy in copies:
        copy.wait()


def vmem_call(body, outs, scratch=()):
    space = pl.BlockSpec(memory_space=pltpu.VMEM)
    return pl.pallas_call(
        body,
        out_shape=outs,
        out_specs=jax.tree.map(lambda _: space, outs),
        scratch_shapes=scratch,
        compiler_params=pltpu.CompilerParams(vmem_limit_bytes=VMEM_BYTES),
        cost_estimate=pl.CostEstimate(flops=0, bytes_accessed=1 << 20, transcendentals=0),
    )


def shape(dims, dtype=BF16):
    return jax.ShapeDtypeStruct(dims, dtype)


def after(value, *others):
    return lax.optimization_barrier((value, *others))[0]


def shards(groups_of, shards_of, inputs, cotangent, weights):
    edge, chans = inputs.shape[1], inputs.shape[4]
    half = edge // 2
    cells = half**3
    count, own_chans = weights.shape[0], weights.shape[1]
    parts = PARTS
    groups = parts // 2
    width = LANES // groups
    values = inputs.reshape(edge**3, chans)
    rows = cotangent.reshape(cotangent.shape[1:])
    row_buffer = [pltpu.VMEM((cells, chans), F32)]

    def across(value, distance):
        return lax.ppermute(value, "dp", [(i, i ^ distance) for i in range(groups_of)])

    def swap(value):
        return lax.ppermute(value, "shard", [(0, 1), (1, 0)])

    def deliver(value, distance):
        pairs = []
        for i in range(groups_of):
            for j in range(shards_of):
                there = i ^ (2 * distance)
                pairs.append((i * shards_of + j, there * shards_of + (j ^ crossing(i % 2, distance))))
        return lax.ppermute(value, ("dp", "shard"), pairs)

    values2, rows2 = across(values, 1), across(rows, 1)
    keep, give = vmem_call(functools.partial(sort_kernel, edge), (shape((8 * cells, LANES)),) * 2)(values)
    *pieces, own, send = vmem_call(
        functools.partial(pack_kernel, edge, groups),
        (shape((8 * cells, LANES)),) * groups + (shape((10 * cells, LANES)),) * 2,
        scratch=row_buffer,
    )(keep, give, rows, values2, rows2)
    got = [deliver(pieces[distance], distance) for distance in DELIVERY]
    other = swap(after(send, *got))
    part, grad = vmem_call(
        functools.partial(sample_kernel, half, False),
        (shape((cells, chans), F32), shape((8 * cells, LANES))),
    )(own, weights)
    *got, part, grad = lax.optimization_barrier((*got, part, grad))
    (back,) = vmem_call(functools.partial(sample_kernel, half, True), (shape((10 * cells, LANES)),))(other, weights)

    splits = (count // 2, count - count // 2)
    totals = []
    for index, taps in enumerate(splits):
        keep, give = vmem_call(
            functools.partial(weight_kernel, half, groups, sum(splits[:index]), taps),
            (shape((taps, width, LANES), F32), shape((taps, width, LANES))),
        )(*got)
        totals.append((keep + across(give, 1).astype(F32)).astype(BF16))
        if index == 0:
            *got, _ = lax.optimization_barrier((*got, totals[0]))
    returned = swap(after(back, totals[0]))
    outputs, input_grad = vmem_call(
        functools.partial(finish_kernel, edge),
        (shape(rows.shape), shape((edge**3, chans))),
        scratch=row_buffer,
    )(part, grad, returned)

    direct = []
    for index, total in enumerate(totals):
        distance = parts
        while distance < groups_of:
            arrived = across(total, distance)
            if index == 1:
                arrived, outputs, input_grad = lax.optimization_barrier((arrived, outputs, input_grad))
            total = (total.astype(F32) + arrived.astype(F32)).astype(BF16)
            distance *= 2
        direct.append([total] + [across(total, distance) for distance in GATHER])
    crossed = [across(jnp.concatenate(values, axis=0), 1) for values in direct]

    def put(base, operands, runs):
        have = [] if base is None else [base]
        return pl.pallas_call(
            functools.partial(place_kernel, parts, width, runs, len(have)),
            in_specs=[pl.BlockSpec(memory_space=pl.ANY)] * len(have)
            + [pl.BlockSpec(memory_space=pltpu.VMEM)] * len(operands),
            out_specs=pl.BlockSpec(memory_space=pl.ANY),
            out_shape=shape((count, own_chans, chans), F32),
            scratch_shapes=[
                pltpu.VMEM((count, own_chans, chans), F32),
                pltpu.SemaphoreType.DMA((len(runs),)),
            ],
            input_output_aliases={0: 0} if have else {},
            compiler_params=pltpu.CompilerParams(vmem_limit_bytes=VMEM_BYTES),
        )(*have, *operands)

    def runs_of(parts_of):
        runs, at = [], 0
        for index, flip in parts_of:
            for low in range(0, splits[index], BLOCK):
                size = min(BLOCK, splits[index] - low)
                pieces = []
                for order, distance in enumerate((0,) + GATHER):
                    place = (at, order * splits[index] + low) if flip else (at + order, low)
                    pieces.append((*place, distance, size))
                runs.append((sum(splits[:index]) + low, flip, pieces))
            at += 1 if flip else 1 + len(GATHER)
        return runs

    early = put(None, [*direct[0], crossed[0], *direct[1]], runs_of([(0, 0), (0, 1), (1, 0)]))
    weight_grad = put(early, [crossed[1]], runs_of([(1, 1)]))
    return outputs.reshape(cotangent.shape), input_grad.reshape(inputs.shape), weight_grad


def build_cols(values):
    edge = values.shape[0]
    half = edge // 2
    width = values.shape[3]
    act = jax.nn.silu(values.astype(jnp.float32)).astype(jnp.bfloat16)
    padded = jnp.pad(act, ((1, 1), (1, 1), (1, 1), (0, 0)))
    pieces = []
    for first in range(3):
        for second in range(3):
            for third in range(3):
                pieces.append(
                    padded[
                        first : first + edge : 2,
                        second : second + edge : 2,
                        third : third + edge : 2,
                    ]
                )
    pieces.append(values[0::2, 0::2, 0::2])
    return jnp.stack(pieces, axis=3).reshape(half * half * half, 28, width)


def spread_back(values, grad_rows, piece, half):
    width = piece.shape[1]
    edge = 2 * half
    grid = jnp.zeros((edge + 2, edge + 2, edge + 2, width), jnp.float32)
    for first in range(3):
        block = jnp.einsum(
            "qo,tco->qtc",
            grad_rows,
            piece[9 * first : 9 * first + 9],
            preferred_element_type=jnp.float32,
        )
        block = block.reshape(half, half, half, 9, width)
        for second in range(3):
            for third in range(3):
                grid = grid.at[
                    first : first + edge : 2, second : second + edge : 2, third : third + edge : 2
                ].add(block[:, :, :, 3 * second + third])
    direct = jnp.einsum(
        "qo,co->qc", grad_rows, piece[27], preferred_element_type=jnp.float32
    ).reshape(half, half, half, width)
    own = values.astype(jnp.float32)
    sigma = jax.nn.sigmoid(own)
    grad_in = grid[1:-1, 1:-1, 1:-1] * sigma * (1.0 + own * (1.0 - sigma))
    grad_in = grad_in.at[0::2, 0::2, 0::2].add(direct)
    return grad_in.astype(jnp.bfloat16)


def general(inputs, cotangent, weights):
    values = inputs[0]
    edge = values.shape[0]
    half = edge // 2
    chans = values.shape[3]
    cols = build_cols(values)
    grad_rows = cotangent[0].reshape(half * half * half, chans)
    result = jnp.einsum(
        "qtc,tco->qo",
        cols,
        lax.all_gather(weights, "shard", axis=1, tiled=True),
        preferred_element_type=jnp.float32,
    )
    grad_in = spread_back(
        values, grad_rows, lax.all_gather(weights, "shard", axis=1, tiled=True), half
    )
    group_values = lax.all_to_all(inputs, "shard", split_axis=4, concat_axis=0, tiled=True)
    group_grads = lax.all_gather(cotangent, "shard", axis=0, tiled=True)
    count = group_values.shape[0]
    group_cols = jax.vmap(build_cols)(group_values)
    group_rows = group_grads.reshape(count, half * half * half, chans)
    per_sample = jnp.einsum(
        "sqtc,sqo->stco", group_cols, group_rows, preferred_element_type=jnp.float32
    )
    owned = jnp.sum(per_sample.astype(jnp.bfloat16).astype(jnp.float32), axis=0)
    weight_grad = lax.psum(owned, "dp")
    outputs = result.astype(jnp.bfloat16).reshape(1, half, half, half, chans)
    return (outputs, grad_in.reshape(1, edge, edge, edge, chans), weight_grad)


def fits(mesh, inputs, cotangent, weights):
    groups_of, shards_of = mesh.shape["dp"], mesh.shape["shard"]
    edge, chans = inputs.shape[1], inputs.shape[4]
    ratio = groups_of // PARTS
    return (
        shards_of == 2
        and chans == shards_of * LANES
        and inputs.shape[0] == groups_of * shards_of
        and inputs.shape[1:4] == (8, 8, 8)
        and groups_of % PARTS == 0
        and ratio & (ratio - 1) == 0
    )


def solution(mesh):
    rows = P(("dp", "shard"), None, None, None, None)
    kernel = P(None, "shard", None)

    def whole(inputs, cotangent, weights):
        body = general
        if fits(mesh, inputs, cotangent, weights):
            body = functools.partial(shards, mesh.shape["dp"], mesh.shape["shard"])
        return jax.shard_map(
            body,
            mesh=mesh,
            in_specs=(rows, rows, kernel),
            out_specs=(rows, rows, kernel),
            check_vma=False,
        )(inputs, cotangent, weights)

    return whole
```

```python
import functools

import jax
import jax.numpy as jnp
from jax import lax
from jax.experimental import pallas as pl
from jax.experimental.pallas import tpu as pltpu
from jax.sharding import PartitionSpec as P

LANES = 128
PARTS = 8
DELIVERY = (1, 2, 3, 0)
GATHER = (2, 4, 6)
BLOCK = 7
VMEM_BYTES = 48 * 1024 * 1024
BF16 = jnp.bfloat16
F32 = jnp.float32

TAP_CLASS = (1, 0, 1)
TAP_SHIFT = (1, 0, 0)


def tap_table():
    table = []
    for first in range(3):
        for second in range(3):
            for third in range(3):
                taps = (first, second, third)
                table.append(
                    (tuple(TAP_CLASS[t] for t in taps), tuple(TAP_SHIFT[t] for t in taps))
                )
    return table


def class_index(parity):
    return 4 * parity[0] + 2 * parity[1] + parity[2]


def dot(left, right, contract=(1, 0)):
    return lax.dot_general(
        left, right, (((contract[0],), (contract[1],)), ((), ())), preferred_element_type=F32
    )


def row_digits(rows, half):
    row = lax.broadcasted_iota(jnp.int32, (rows, 1), 0)
    return (row // (half * half)) % half, (row // half) % half, row % half


def shift_rows(value, shift, half, forward):
    if not any(shift):
        return value
    rows = value.shape[0]
    offset = (shift[0] * half + shift[1]) * half + shift[2]
    keep = None
    for digit, step in zip(row_digits(rows, half), shift):
        if step:
            inside = digit >= step if forward else digit < half - step
            keep = inside if keep is None else keep & inside
    moved = pltpu.roll(value, offset if forward else rows - offset, 0)
    return jnp.where(keep, moved, 0.0)


def plane_order(edge, blocks):
    half = edge // 2
    plane = edge * edge
    size = blocks * plane
    row = lax.broadcasted_iota(jnp.int32, (size, size), 0)
    col = lax.broadcasted_iota(jnp.int32, (size, size), 1)
    inner = row % plane
    parity, cell = inner // (half * half), inner % (half * half)
    second = 2 * (cell // half) + parity // 2
    third = 2 * (cell % half) + parity % 2
    return (col == (row // plane) * plane + second * edge + third).astype(BF16)


def rows_in(rows_ref, cot_ref, half):
    for i in range(half):
        for j in range(half):
            start = (i * half + j) * half
            rows_ref[start : start + half, :] = cot_ref[i, j].astype(F32)
    return rows_ref[...].astype(BF16)


def sorted_cells(edge, ref):
    half = edge // 2
    hh, plane = half * half, edge * edge
    blocks = 256 // plane
    order = plane_order(edge, blocks)
    planes = []
    for start in range(0, edge, blocks):
        moved = dot(order, ref[start * plane : (start + blocks) * plane, :]).astype(BF16)
        planes += [moved[b * plane : (b + 1) * plane] for b in range(blocks)]
    return [
        jnp.concatenate([planes[2 * i + first][inner * hh : (inner + 1) * hh] for i in range(half)], axis=0)
        for first in range(2)
        for inner in range(4)
    ]


def put_cots(ref, start, cots):
    cells = cots.shape[0]
    for side in range(2):
        ref[start + side * cells : start + (side + 1) * cells, :] = cots[:, side * LANES : (side + 1) * LANES]


def sort_kernel(edge, x_ref, keep_ref, send_ref):
    cells = (edge // 2) ** 3
    here = lax.axis_index("shard")
    for index, value in enumerate(sorted_cells(edge, x_ref)):
        low, high = value[:, :LANES], value[:, LANES:]
        keep_ref[index * cells : (index + 1) * cells, :] = jnp.where(here == 0, low, high)
        send_ref[index * cells : (index + 1) * cells, :] = jnp.where(here == 0, high, low)


def crossing(core, distance):
    return core ^ (bin(distance).count("1") % 2)


def pack_kernel(edge, groups, keep_ref, give_ref, cot_ref, x2_ref, cot2_ref, *refs):
    piece_refs, (own_ref, send_ref, rows_ref) = refs[:groups], refs[groups:]
    half = edge // 2
    cells = half**3
    width = LANES // groups
    place = lax.axis_index("dp")
    core, group = lax.rem(place, 2), lax.rem(place // 2, groups)
    here = lax.axis_index("shard")
    second = sorted_cells(edge, x2_ref)
    size = 4 * LANES
    row = lax.broadcasted_iota(jnp.int32, (size, size), 0)
    col = lax.broadcasted_iota(jnp.int32, (size, size), 1)
    source = ((col // width) % 4) * LANES + (col // LANES) * width + col % width
    lane_order = (row == source).astype(BF16)
    packed = []
    for ref, owner in ((keep_ref, here), (give_ref, 1 - here)):
        samples = [
            [ref[index * cells : (index + 1) * cells, :] for index in range(8)],
            [jnp.where(owner == 0, value[:, :LANES], value[:, LANES:]) for value in second],
        ]
        wide = jnp.concatenate(
            [
                jnp.concatenate(classes[4 * first : 4 * first + 4], axis=1)
                for classes in samples
                for first in range(2)
            ],
            axis=0,
        )
        packed.append(dot(wide, lane_order).astype(BF16))
    cots = [rows_in(rows_ref, ref, half) for ref in (cot_ref, cot2_ref)]
    for distance, ref in enumerate(piece_refs):
        owner = group ^ distance
        chosen = jnp.where(crossing(core, distance) == 0, packed[0], packed[1])
        value = chosen[:, (groups - 1) * LANES :]
        for index in range(groups - 1):
            value = jnp.where(owner == index, chosen[:, index * LANES : (index + 1) * LANES], value)
        ref[0 : 4 * cells, :] = value
        put_cots(ref, 4 * cells, cots[0])
        put_cots(ref, 6 * cells, cots[1])
    for ref, half_ref in ((own_ref, keep_ref), (send_ref, give_ref)):
        ref[0 : 8 * cells, :] = half_ref[...]
        put_cots(ref, 8 * cells, cots[0])


def weight_kernel(half, groups, start, count, *refs):
    got_refs, (keep_ref, give_ref) = refs[:groups], refs[groups:]
    cells = half**3
    width = LANES // groups
    chans = 2 * LANES
    core = lax.rem(lax.axis_index("dp"), 2)
    table = tap_table()
    wanted = range(start, start + count)
    needs = {(table[tap][0][0], table[tap][1][0]) for tap in wanted if tap < len(table)}

    def gather(offset):
        return jnp.concatenate(
            [ref[start : start + cells, :] for ref in got_refs for start in offset], axis=0
        )

    raw, acts = {}, {}
    for first in range(2):
        raw[first] = gather([first * cells, (2 + first) * cells])
        wide = raw[first].astype(F32)
        acts[first] = (wide / (1.0 + jnp.exp(-wide))).astype(BF16)
    cots = jnp.concatenate(
        [gather([(4 + side) * cells, (6 + side) * cells]) for side in range(2)], axis=1
    )
    sums = {}
    for si in range(2):
        firsts = [first for first in range(2) if (first, si) in needs]
        if firsts:
            right = jnp.concatenate(
                [
                    shift_rows(cots.astype(F32), (si, sj, sk), half, False).astype(BF16)
                    for sj in range(2)
                    for sk in range(2)
                ],
                axis=1,
            )
            for first in firsts:
                sums[first, si] = dot(acts[first], right, (0, 0))
    for tap in wanted:
        if tap < len(table):
            parity, shift = table[tap]
            row = (2 * parity[1] + parity[2]) * width
            col = (2 * shift[1] + shift[2]) * chans
            value = sums[parity[0], shift[0]][row : row + width, col : col + chans]
        else:
            value = dot(raw[0], cots, (0, 0))[:width]
        low, high = value[:, :LANES], value[:, LANES:]
        keep_ref[tap - start] = jnp.where(core == 0, low, high)
        give_ref[tap - start] = jnp.where(core == 0, high, low).astype(BF16)


def sample_kernel(half, give, own_ref, w_ref, *refs):
    grad_ref = refs[-1]
    cells = half**3
    count = len(tap_table())
    cots = jnp.concatenate([own_ref[(8 + side) * cells : (9 + side) * cells, :] for side in range(2)], axis=1).astype(F32)
    moved, gathered = {}, {}
    shifts = [(si, sj, sk) for si in range(2) for sj in range(2) for sk in range(2)]
    for shift in shifts:
        moved[shift] = shift_rows(cots, shift, half, False).astype(BF16)
    for index in range(8):
        rows = slice(index * cells, (index + 1) * cells)
        value = own_ref[rows, :]
        wide = value.astype(F32)
        sigma = 1.0 / (1.0 + jnp.exp(-wide))
        act = (wide * sigma).astype(BF16)
        back = None
        for tap, (parity, shift) in enumerate(tap_table()):
            if class_index(parity) != index:
                continue
            weight = w_ref[tap]
            term = dot(act, weight)
            gathered[shift] = term if shift not in gathered else gathered[shift] + term
            term = dot(moved[shift], weight, (1, 1))
            back = term if back is None else back + term
        grad = back * sigma * (1.0 + wide * (1.0 - sigma))
        if index == 0:
            weight = w_ref[count]
            gathered[0, 0, 0] = gathered[0, 0, 0] + dot(value, weight)
            grad = grad + dot(moved[0, 0, 0], weight, (1, 1))
        grad_ref[rows, :] = grad.astype(BF16)
    total = gathered[0, 0, 0]
    for shift in shifts[1:]:
        total = total + shift_rows(gathered[shift], shift, half, True)
    if give:
        put_cots(grad_ref, 8 * cells, total.astype(BF16))
    else:
        refs[0][...] = total


def finish_kernel(edge, part_ref, grad_ref, got_ref, out_ref, back_ref, rows_ref):
    half = edge // 2
    hh, cells, plane = half * half, half**3, edge * edge
    here = lax.axis_index("shard")
    got = jnp.concatenate(
        [got_ref[8 * cells : 9 * cells, :], got_ref[9 * cells : 10 * cells, :]], axis=1
    )
    rows_ref[...] = part_ref[...] + got.astype(F32)
    for i in range(half):
        for j in range(half):
            start = (i * half + j) * half
            out_ref[i, j] = rows_ref[start : start + half, :].astype(BF16)
    mine, theirs = grad_ref[...], got_ref[0 : 8 * cells, :]
    wide = jnp.concatenate(
        [jnp.where(here == 0, mine, theirs), jnp.where(here == 0, theirs, mine)], axis=1
    )
    blocks = 256 // plane
    order = plane_order(edge, blocks)
    for start in range(0, edge, blocks):
        pieces = []
        for b in range(blocks):
            first, i = (start + b) % 2, (start + b) // 2
            for inner in range(4):
                row = (4 * first + inner) * cells + i * hh
                pieces.append(wide[row : row + hh])
        back_ref[start * plane : (start + blocks) * plane, :] = dot(
            order, jnp.concatenate(pieces, axis=0), (0, 0)
        ).astype(BF16)


def place_kernel(parts, width, runs, has_base, *refs):
    out_ref, buffer, sem = refs[-3:]
    refs = refs[has_base:-3]
    place = lax.axis_index("dp")
    part = lax.rem(place, parts)
    copies = []
    for slot, (start, flip, pieces) in enumerate(runs):
        count = pieces[0][3]
        for index, offset, distance, _ in pieces:
            group = (part ^ distance) // 2
            rows = pl.ds(pl.multiple_of(group * width, width), width)
            buffer[start : start + count, rows, flip * LANES : (flip + 1) * LANES] = refs[index][
                offset : offset + count
            ].astype(F32)
        side = lax.rem(place, 2) ^ flip
        cols = pl.ds(pl.multiple_of(side * LANES, LANES), LANES)
        copy = pltpu.make_async_copy(
            buffer.at[start : start + count, :, flip * LANES : (flip + 1) * LANES],
            out_ref.at[start : start + count, :, cols],
            sem.at[slot],
        )
        copy.start()
        copies.append(copy)
    for copy in copies:
        copy.wait()


def vmem_call(body, outs, scratch=()):
    space = pl.BlockSpec(memory_space=pltpu.VMEM)
    return pl.pallas_call(
        body,
        out_shape=outs,
        out_specs=jax.tree.map(lambda _: space, outs),
        scratch_shapes=scratch,
        compiler_params=pltpu.CompilerParams(vmem_limit_bytes=VMEM_BYTES),
        cost_estimate=pl.CostEstimate(flops=0, bytes_accessed=1 << 20, transcendentals=0),
    )


def shape(dims, dtype=BF16):
    return jax.ShapeDtypeStruct(dims, dtype)


def after(value, *others):
    return lax.optimization_barrier((value, *others))[0]


def shards(groups_of, shards_of, inputs, cotangent, weights):
    edge, chans = inputs.shape[1], inputs.shape[4]
    half = edge // 2
    cells = half**3
    count, own_chans = weights.shape[0], weights.shape[1]
    parts = PARTS
    groups = parts // 2
    width = LANES // groups
    values = inputs.reshape(edge**3, chans)
    rows = cotangent.reshape(cotangent.shape[1:])
    row_buffer = [pltpu.VMEM((cells, chans), F32)]

    def across(value, distance):
        return lax.ppermute(value, "dp", [(i, i ^ distance) for i in range(groups_of)])

    def swap(value):
        return lax.ppermute(value, "shard", [(0, 1), (1, 0)])

    def deliver(value, distance):
        pairs = []
        for i in range(groups_of):
            for j in range(shards_of):
                there = i ^ (2 * distance)
                pairs.append((i * shards_of + j, there * shards_of + (j ^ crossing(i % 2, distance))))
        return lax.ppermute(value, ("dp", "shard"), pairs)

    values2, rows2 = across(values, 1), across(rows, 1)
    keep, give = vmem_call(functools.partial(sort_kernel, edge), (shape((8 * cells, LANES)),) * 2)(values)
    *pieces, own, send = vmem_call(
        functools.partial(pack_kernel, edge, groups),
        (shape((8 * cells, LANES)),) * groups + (shape((10 * cells, LANES)),) * 2,
        scratch=row_buffer,
    )(keep, give, rows, values2, rows2)
    got = [deliver(pieces[distance], distance) for distance in DELIVERY]
    other = swap(after(send, *got))
    part, grad = vmem_call(
        functools.partial(sample_kernel, half, False),
        (shape((cells, chans), F32), shape((8 * cells, LANES))),
    )(own, weights)
    *got, part, grad = lax.optimization_barrier((*got, part, grad))
    (back,) = vmem_call(functools.partial(sample_kernel, half, True), (shape((10 * cells, LANES)),))(other, weights)

    splits = (count // 2 + 1, count - count // 2 - 1)
    totals = []
    for index, taps in enumerate(splits):
        keep, give = vmem_call(
            functools.partial(weight_kernel, half, groups, sum(splits[:index]), taps),
            (shape((taps, width, LANES), F32), shape((taps, width, LANES))),
        )(*got)
        totals.append((keep + across(give, 1).astype(F32)).astype(BF16))
        if index == 0:
            *got, _ = lax.optimization_barrier((*got, totals[0]))
    returned = swap(after(back, totals[0]))
    outputs, input_grad = vmem_call(
        functools.partial(finish_kernel, edge),
        (shape(rows.shape), shape((edge**3, chans))),
        scratch=row_buffer,
    )(part, grad, returned)

    direct = []
    for index, total in enumerate(totals):
        distance = parts
        while distance < groups_of:
            arrived = across(total, distance)
            if index == 1:
                arrived, outputs, input_grad = lax.optimization_barrier((arrived, outputs, input_grad))
            total = (total.astype(F32) + arrived.astype(F32)).astype(BF16)
            distance *= 2
        direct.append([total] + [across(total, distance) for distance in GATHER])
    crossed = [across(jnp.concatenate(values, axis=0), 1) for values in direct]

    def put(base, operands, runs):
        have = [] if base is None else [base]
        return pl.pallas_call(
            functools.partial(place_kernel, parts, width, runs, len(have)),
            in_specs=[pl.BlockSpec(memory_space=pl.ANY)] * len(have)
            + [pl.BlockSpec(memory_space=pltpu.VMEM)] * len(operands),
            out_specs=pl.BlockSpec(memory_space=pl.ANY),
            out_shape=shape((count, own_chans, chans), F32),
            scratch_shapes=[
                pltpu.VMEM((count, own_chans, chans), F32),
                pltpu.SemaphoreType.DMA((len(runs),)),
            ],
            input_output_aliases={0: 0} if have else {},
            compiler_params=pltpu.CompilerParams(vmem_limit_bytes=VMEM_BYTES),
        )(*have, *operands)

    def runs_of(parts_of):
        runs, at = [], 0
        for index, flip in parts_of:
            for low in range(0, splits[index], BLOCK):
                size = min(BLOCK, splits[index] - low)
                pieces = []
                for order, distance in enumerate((0,) + GATHER):
                    place = (at, order * splits[index] + low) if flip else (at + order, low)
                    pieces.append((*place, distance, size))
                runs.append((sum(splits[:index]) + low, flip, pieces))
            at += 1 if flip else 1 + len(GATHER)
        return runs

    early = put(None, [*direct[0], crossed[0], *direct[1]], runs_of([(0, 0), (0, 1), (1, 0)]))
    weight_grad = put(early, [crossed[1]], runs_of([(1, 1)]))
    return outputs.reshape(cotangent.shape), input_grad.reshape(inputs.shape), weight_grad


def build_cols(values):
    edge = values.shape[0]
    half = edge // 2
    width = values.shape[3]
    act = jax.nn.silu(values.astype(jnp.float32)).astype(jnp.bfloat16)
    padded = jnp.pad(act, ((1, 1), (1, 1), (1, 1), (0, 0)))
    pieces = []
    for first in range(3):
        for second in range(3):
            for third in range(3):
                pieces.append(
                    padded[
                        first : first + edge : 2,
                        second : second + edge : 2,
                        third : third + edge : 2,
                    ]
                )
    pieces.append(values[0::2, 0::2, 0::2])
    return jnp.stack(pieces, axis=3).reshape(half * half * half, 28, width)


def spread_back(values, grad_rows, piece, half):
    width = piece.shape[1]
    edge = 2 * half
    grid = jnp.zeros((edge + 2, edge + 2, edge + 2, width), jnp.float32)
    for first in range(3):
        block = jnp.einsum(
            "qo,tco->qtc",
            grad_rows,
            piece[9 * first : 9 * first + 9],
            preferred_element_type=jnp.float32,
        )
        block = block.reshape(half, half, half, 9, width)
        for second in range(3):
            for third in range(3):
                grid = grid.at[
                    first : first + edge : 2, second : second + edge : 2, third : third + edge : 2
                ].add(block[:, :, :, 3 * second + third])
    direct = jnp.einsum(
        "qo,co->qc", grad_rows, piece[27], preferred_element_type=jnp.float32
    ).reshape(half, half, half, width)
    own = values.astype(jnp.float32)
    sigma = jax.nn.sigmoid(own)
    grad_in = grid[1:-1, 1:-1, 1:-1] * sigma * (1.0 + own * (1.0 - sigma))
    grad_in = grad_in.at[0::2, 0::2, 0::2].add(direct)
    return grad_in.astype(jnp.bfloat16)


def general(inputs, cotangent, weights):
    values = inputs[0]
    edge = values.shape[0]
    half = edge // 2
    chans = values.shape[3]
    cols = build_cols(values)
    grad_rows = cotangent[0].reshape(half * half * half, chans)
    result = jnp.einsum(
        "qtc,tco->qo",
        cols,
        lax.all_gather(weights, "shard", axis=1, tiled=True),
        preferred_element_type=jnp.float32,
    )
    grad_in = spread_back(
        values, grad_rows, lax.all_gather(weights, "shard", axis=1, tiled=True), half
    )
    group_values = lax.all_to_all(inputs, "shard", split_axis=4, concat_axis=0, tiled=True)
    group_grads = lax.all_gather(cotangent, "shard", axis=0, tiled=True)
    count = group_values.shape[0]
    group_cols = jax.vmap(build_cols)(group_values)
    group_rows = group_grads.reshape(count, half * half * half, chans)
    per_sample = jnp.einsum(
        "sqtc,sqo->stco", group_cols, group_rows, preferred_element_type=jnp.float32
    )
    owned = jnp.sum(per_sample.astype(jnp.bfloat16).astype(jnp.float32), axis=0)
    weight_grad = lax.psum(owned, "dp")
    outputs = result.astype(jnp.bfloat16).reshape(1, half, half, half, chans)
    return (outputs, grad_in.reshape(1, edge, edge, edge, chans), weight_grad)


def fits(mesh, inputs, cotangent, weights):
    groups_of, shards_of = mesh.shape["dp"], mesh.shape["shard"]
    edge, chans = inputs.shape[1], inputs.shape[4]
    ratio = groups_of // PARTS
    return (
        shards_of == 2
        and chans == shards_of * LANES
        and inputs.shape[0] == groups_of * shards_of
        and inputs.shape[1:4] == (8, 8, 8)
        and groups_of % PARTS == 0
        and ratio & (ratio - 1) == 0
    )


def solution(mesh):
    rows = P(("dp", "shard"), None, None, None, None)
    kernel = P(None, "shard", None)

    def whole(inputs, cotangent, weights):
        body = general
        if fits(mesh, inputs, cotangent, weights):
            body = functools.partial(shards, mesh.shape["dp"], mesh.shape["shard"])
        return jax.shard_map(
            body,
            mesh=mesh,
            in_specs=(rows, rows, kernel),
            out_specs=(rows, rows, kernel),
            check_vma=False,
        )(inputs, cotangent, weights)

    return whole
```

```python
import functools

import jax
import jax.numpy as jnp
from jax import lax
from jax.experimental import pallas as pl
from jax.experimental.pallas import tpu as pltpu
from jax.sharding import PartitionSpec as P

LANES = 128
PARTS = 8
DELIVERY = (1, 2, 3, 0)
GATHER = (4, 2, 6)
BLOCK = 7
VMEM_BYTES = 48 * 1024 * 1024
BF16 = jnp.bfloat16
F32 = jnp.float32

TAP_CLASS = (1, 0, 1)
TAP_SHIFT = (1, 0, 0)


def tap_table():
    table = []
    for first in range(3):
        for second in range(3):
            for third in range(3):
                taps = (first, second, third)
                table.append(
                    (tuple(TAP_CLASS[t] for t in taps), tuple(TAP_SHIFT[t] for t in taps))
                )
    return table


def class_index(parity):
    return 4 * parity[0] + 2 * parity[1] + parity[2]


def dot(left, right, contract=(1, 0)):
    return lax.dot_general(
        left, right, (((contract[0],), (contract[1],)), ((), ())), preferred_element_type=F32
    )


def row_digits(rows, half):
    row = lax.broadcasted_iota(jnp.int32, (rows, 1), 0)
    return (row // (half * half)) % half, (row // half) % half, row % half


def shift_rows(value, shift, half, forward):
    if not any(shift):
        return value
    rows = value.shape[0]
    offset = (shift[0] * half + shift[1]) * half + shift[2]
    keep = None
    for digit, step in zip(row_digits(rows, half), shift):
        if step:
            inside = digit >= step if forward else digit < half - step
            keep = inside if keep is None else keep & inside
    moved = pltpu.roll(value, offset if forward else rows - offset, 0)
    return jnp.where(keep, moved, 0.0)


def plane_order(edge, blocks):
    half = edge // 2
    plane = edge * edge
    size = blocks * plane
    row = lax.broadcasted_iota(jnp.int32, (size, size), 0)
    col = lax.broadcasted_iota(jnp.int32, (size, size), 1)
    inner = row % plane
    parity, cell = inner // (half * half), inner % (half * half)
    second = 2 * (cell // half) + parity // 2
    third = 2 * (cell % half) + parity % 2
    return (col == (row // plane) * plane + second * edge + third).astype(BF16)


def rows_in(rows_ref, cot_ref, half):
    for i in range(half):
        for j in range(half):
            start = (i * half + j) * half
            rows_ref[start : start + half, :] = cot_ref[i, j].astype(F32)
    return rows_ref[...].astype(BF16)


def sorted_cells(edge, ref):
    half = edge // 2
    hh, plane = half * half, edge * edge
    blocks = 256 // plane
    order = plane_order(edge, blocks)
    planes = []
    for start in range(0, edge, blocks):
        moved = dot(order, ref[start * plane : (start + blocks) * plane, :]).astype(BF16)
        planes += [moved[b * plane : (b + 1) * plane] for b in range(blocks)]
    return [
        jnp.concatenate([planes[2 * i + first][inner * hh : (inner + 1) * hh] for i in range(half)], axis=0)
        for first in range(2)
        for inner in range(4)
    ]


def put_cots(ref, start, cots):
    cells = cots.shape[0]
    for side in range(2):
        ref[start + side * cells : start + (side + 1) * cells, :] = cots[:, side * LANES : (side + 1) * LANES]


def sort_kernel(edge, x_ref, keep_ref, send_ref):
    cells = (edge // 2) ** 3
    here = lax.axis_index("shard")
    for index, value in enumerate(sorted_cells(edge, x_ref)):
        low, high = value[:, :LANES], value[:, LANES:]
        keep_ref[index * cells : (index + 1) * cells, :] = jnp.where(here == 0, low, high)
        send_ref[index * cells : (index + 1) * cells, :] = jnp.where(here == 0, high, low)


def crossing(core, distance):
    return core ^ (bin(distance).count("1") % 2)


def pack_kernel(edge, groups, keep_ref, give_ref, cot_ref, x2_ref, cot2_ref, *refs):
    piece_refs, (own_ref, send_ref, rows_ref) = refs[:groups], refs[groups:]
    half = edge // 2
    cells = half**3
    width = LANES // groups
    place = lax.axis_index("dp")
    core, group = lax.rem(place, 2), lax.rem(place // 2, groups)
    here = lax.axis_index("shard")
    second = sorted_cells(edge, x2_ref)
    size = 4 * LANES
    row = lax.broadcasted_iota(jnp.int32, (size, size), 0)
    col = lax.broadcasted_iota(jnp.int32, (size, size), 1)
    source = ((col // width) % 4) * LANES + (col // LANES) * width + col % width
    lane_order = (row == source).astype(BF16)
    packed = []
    for ref, owner in ((keep_ref, here), (give_ref, 1 - here)):
        samples = [
            [ref[index * cells : (index + 1) * cells, :] for index in range(8)],
            [jnp.where(owner == 0, value[:, :LANES], value[:, LANES:]) for value in second],
        ]
        wide = jnp.concatenate(
            [
                jnp.concatenate(classes[4 * first : 4 * first + 4], axis=1)
                for classes in samples
                for first in range(2)
            ],
            axis=0,
        )
        packed.append(dot(wide, lane_order).astype(BF16))
    cots = [rows_in(rows_ref, ref, half) for ref in (cot_ref, cot2_ref)]
    for distance, ref in enumerate(piece_refs):
        owner = group ^ distance
        chosen = jnp.where(crossing(core, distance) == 0, packed[0], packed[1])
        value = chosen[:, (groups - 1) * LANES :]
        for index in range(groups - 1):
            value = jnp.where(owner == index, chosen[:, index * LANES : (index + 1) * LANES], value)
        ref[0 : 4 * cells, :] = value
        put_cots(ref, 4 * cells, cots[0])
        put_cots(ref, 6 * cells, cots[1])
    for ref, half_ref in ((own_ref, keep_ref), (send_ref, give_ref)):
        ref[0 : 8 * cells, :] = half_ref[...]
        put_cots(ref, 8 * cells, cots[0])


def weight_kernel(half, groups, start, count, *refs):
    got_refs, (keep_ref, give_ref) = refs[:groups], refs[groups:]
    cells = half**3
    width = LANES // groups
    chans = 2 * LANES
    core = lax.rem(lax.axis_index("dp"), 2)
    table = tap_table()
    wanted = range(start, start + count)
    needs = {(table[tap][0][0], table[tap][1][0]) for tap in wanted if tap < len(table)}

    def gather(offset):
        return jnp.concatenate(
            [ref[start : start + cells, :] for ref in got_refs for start in offset], axis=0
        )

    raw, acts = {}, {}
    for first in range(2):
        raw[first] = gather([first * cells, (2 + first) * cells])
        wide = raw[first].astype(F32)
        acts[first] = (wide / (1.0 + jnp.exp(-wide))).astype(BF16)
    cots = jnp.concatenate(
        [gather([(4 + side) * cells, (6 + side) * cells]) for side in range(2)], axis=1
    )
    sums = {}
    for si in range(2):
        firsts = [first for first in range(2) if (first, si) in needs]
        if firsts:
            right = jnp.concatenate(
                [
                    shift_rows(cots.astype(F32), (si, sj, sk), half, False).astype(BF16)
                    for sj in range(2)
                    for sk in range(2)
                ],
                axis=1,
            )
            for first in firsts:
                sums[first, si] = dot(acts[first], right, (0, 0))
    for tap in wanted:
        if tap < len(table):
            parity, shift = table[tap]
            row = (2 * parity[1] + parity[2]) * width
            col = (2 * shift[1] + shift[2]) * chans
            value = sums[parity[0], shift[0]][row : row + width, col : col + chans]
        else:
            value = dot(raw[0], cots, (0, 0))[:width]
        low, high = value[:, :LANES], value[:, LANES:]
        keep_ref[tap - start] = jnp.where(core == 0, low, high)
        give_ref[tap - start] = jnp.where(core == 0, high, low).astype(BF16)


def sample_kernel(half, give, own_ref, w_ref, *refs):
    grad_ref = refs[-1]
    cells = half**3
    count = len(tap_table())
    cots = jnp.concatenate([own_ref[(8 + side) * cells : (9 + side) * cells, :] for side in range(2)], axis=1).astype(F32)
    moved, gathered = {}, {}
    shifts = [(si, sj, sk) for si in range(2) for sj in range(2) for sk in range(2)]
    for shift in shifts:
        moved[shift] = shift_rows(cots, shift, half, False).astype(BF16)
    for index in range(8):
        rows = slice(index * cells, (index + 1) * cells)
        value = own_ref[rows, :]
        wide = value.astype(F32)
        sigma = 1.0 / (1.0 + jnp.exp(-wide))
        act = (wide * sigma).astype(BF16)
        back = None
        for tap, (parity, shift) in enumerate(tap_table()):
            if class_index(parity) != index:
                continue
            weight = w_ref[tap]
            term = dot(act, weight)
            gathered[shift] = term if shift not in gathered else gathered[shift] + term
            term = dot(moved[shift], weight, (1, 1))
            back = term if back is None else back + term
        grad = back * sigma * (1.0 + wide * (1.0 - sigma))
        if index == 0:
            weight = w_ref[count]
            gathered[0, 0, 0] = gathered[0, 0, 0] + dot(value, weight)
            grad = grad + dot(moved[0, 0, 0], weight, (1, 1))
        grad_ref[rows, :] = grad.astype(BF16)
    total = gathered[0, 0, 0]
    for shift in shifts[1:]:
        total = total + shift_rows(gathered[shift], shift, half, True)
    if give:
        put_cots(grad_ref, 8 * cells, total.astype(BF16))
    else:
        refs[0][...] = total


def finish_kernel(edge, part_ref, grad_ref, got_ref, out_ref, back_ref, rows_ref):
    half = edge // 2
    hh, cells, plane = half * half, half**3, edge * edge
    here = lax.axis_index("shard")
    got = jnp.concatenate(
        [got_ref[8 * cells : 9 * cells, :], got_ref[9 * cells : 10 * cells, :]], axis=1
    )
    rows_ref[...] = part_ref[...] + got.astype(F32)
    for i in range(half):
        for j in range(half):
            start = (i * half + j) * half
            out_ref[i, j] = rows_ref[start : start + half, :].astype(BF16)
    mine, theirs = grad_ref[...], got_ref[0 : 8 * cells, :]
    wide = jnp.concatenate(
        [jnp.where(here == 0, mine, theirs), jnp.where(here == 0, theirs, mine)], axis=1
    )
    blocks = 256 // plane
    order = plane_order(edge, blocks)
    for start in range(0, edge, blocks):
        pieces = []
        for b in range(blocks):
            first, i = (start + b) % 2, (start + b) // 2
            for inner in range(4):
                row = (4 * first + inner) * cells + i * hh
                pieces.append(wide[row : row + hh])
        back_ref[start * plane : (start + blocks) * plane, :] = dot(
            order, jnp.concatenate(pieces, axis=0), (0, 0)
        ).astype(BF16)


def place_kernel(parts, width, runs, has_base, *refs):
    out_ref, buffer, sem = refs[-3:]
    refs = refs[has_base:-3]
    place = lax.axis_index("dp")
    part = lax.rem(place, parts)
    copies = []
    for slot, (start, flip, pieces) in enumerate(runs):
        count = pieces[0][3]
        for index, offset, distance, _ in pieces:
            group = (part ^ distance) // 2
            rows = pl.ds(pl.multiple_of(group * width, width), width)
            buffer[start : start + count, rows, flip * LANES : (flip + 1) * LANES] = refs[index][
                offset : offset + count
            ].astype(F32)
        side = lax.rem(place, 2) ^ flip
        cols = pl.ds(pl.multiple_of(side * LANES, LANES), LANES)
        copy = pltpu.make_async_copy(
            buffer.at[start : start + count, :, flip * LANES : (flip + 1) * LANES],
            out_ref.at[start : start + count, :, cols],
            sem.at[slot],
        )
        copy.start()
        copies.append(copy)
    for copy in copies:
        copy.wait()


def vmem_call(body, outs, scratch=()):
    space = pl.BlockSpec(memory_space=pltpu.VMEM)
    return pl.pallas_call(
        body,
        out_shape=outs,
        out_specs=jax.tree.map(lambda _: space, outs),
        scratch_shapes=scratch,
        compiler_params=pltpu.CompilerParams(vmem_limit_bytes=VMEM_BYTES),
        cost_estimate=pl.CostEstimate(flops=0, bytes_accessed=1 << 20, transcendentals=0),
    )


def shape(dims, dtype=BF16):
    return jax.ShapeDtypeStruct(dims, dtype)


def after(value, *others):
    return lax.optimization_barrier((value, *others))[0]


def shards(groups_of, shards_of, inputs, cotangent, weights):
    edge, chans = inputs.shape[1], inputs.shape[4]
    half = edge // 2
    cells = half**3
    count, own_chans = weights.shape[0], weights.shape[1]
    parts = PARTS
    groups = parts // 2
    width = LANES // groups
    values = inputs.reshape(edge**3, chans)
    rows = cotangent.reshape(cotangent.shape[1:])
    row_buffer = [pltpu.VMEM((cells, chans), F32)]

    def across(value, distance):
        return lax.ppermute(value, "dp", [(i, i ^ distance) for i in range(groups_of)])

    def swap(value):
        return lax.ppermute(value, "shard", [(0, 1), (1, 0)])

    def deliver(value, distance):
        pairs = []
        for i in range(groups_of):
            for j in range(shards_of):
                there = i ^ (2 * distance)
                pairs.append((i * shards_of + j, there * shards_of + (j ^ crossing(i % 2, distance))))
        return lax.ppermute(value, ("dp", "shard"), pairs)

    values2, rows2 = across(values, 1), across(rows, 1)
    keep, give = vmem_call(functools.partial(sort_kernel, edge), (shape((8 * cells, LANES)),) * 2)(values)
    *pieces, own, send = vmem_call(
        functools.partial(pack_kernel, edge, groups),
        (shape((8 * cells, LANES)),) * groups + (shape((10 * cells, LANES)),) * 2,
        scratch=row_buffer,
    )(keep, give, rows, values2, rows2)
    got = [deliver(pieces[distance], distance) for distance in DELIVERY]
    other = swap(after(send, *got))
    part, grad = vmem_call(
        functools.partial(sample_kernel, half, False),
        (shape((cells, chans), F32), shape((8 * cells, LANES))),
    )(own, weights)
    *got, part, grad = lax.optimization_barrier((*got, part, grad))
    (back,) = vmem_call(functools.partial(sample_kernel, half, True), (shape((10 * cells, LANES)),))(other, weights)

    splits = (count // 2 + 1, count - count // 2 - 1)
    totals = []
    for index, taps in enumerate(splits):
        keep, give = vmem_call(
            functools.partial(weight_kernel, half, groups, sum(splits[:index]), taps),
            (shape((taps, width, LANES), F32), shape((taps, width, LANES))),
        )(*got)
        totals.append((keep + across(give, 1).astype(F32)).astype(BF16))
        if index == 0:
            *got, _ = lax.optimization_barrier((*got, totals[0]))
    returned = swap(after(back, totals[0]))
    outputs, input_grad = vmem_call(
        functools.partial(finish_kernel, edge),
        (shape(rows.shape), shape((edge**3, chans))),
        scratch=row_buffer,
    )(part, grad, returned)

    direct = []
    for index, total in enumerate(totals):
        distance = parts
        while distance < groups_of:
            arrived = across(total, distance)
            if index == 1:
                arrived, outputs, input_grad = lax.optimization_barrier((arrived, outputs, input_grad))
            total = (total.astype(F32) + arrived.astype(F32)).astype(BF16)
            distance *= 2
        direct.append([total] + [across(total, distance) for distance in GATHER])
    crossed = [across(jnp.concatenate(values, axis=0), 1) for values in direct]

    def put(base, operands, runs):
        have = [] if base is None else [base]
        return pl.pallas_call(
            functools.partial(place_kernel, parts, width, runs, len(have)),
            in_specs=[pl.BlockSpec(memory_space=pl.ANY)] * len(have)
            + [pl.BlockSpec(memory_space=pltpu.VMEM)] * len(operands),
            out_specs=pl.BlockSpec(memory_space=pl.ANY),
            out_shape=shape((count, own_chans, chans), F32),
            scratch_shapes=[
                pltpu.VMEM((count, own_chans, chans), F32),
                pltpu.SemaphoreType.DMA((len(runs),)),
            ],
            input_output_aliases={0: 0} if have else {},
            compiler_params=pltpu.CompilerParams(vmem_limit_bytes=VMEM_BYTES),
        )(*have, *operands)

    def runs_of(parts_of):
        runs, at = [], 0
        for index, flip in parts_of:
            for low in range(0, splits[index], BLOCK):
                size = min(BLOCK, splits[index] - low)
                pieces = []
                for order, distance in enumerate((0,) + GATHER):
                    place = (at, order * splits[index] + low) if flip else (at + order, low)
                    pieces.append((*place, distance, size))
                runs.append((sum(splits[:index]) + low, flip, pieces))
            at += 1 if flip else 1 + len(GATHER)
        return runs

    early = put(None, [*direct[0], crossed[0], *direct[1]], runs_of([(0, 0), (0, 1), (1, 0)]))
    weight_grad = put(early, [crossed[1]], runs_of([(1, 1)]))
    return outputs.reshape(cotangent.shape), input_grad.reshape(inputs.shape), weight_grad


def build_cols(values):
    edge = values.shape[0]
    half = edge // 2
    width = values.shape[3]
    act = jax.nn.silu(values.astype(jnp.float32)).astype(jnp.bfloat16)
    padded = jnp.pad(act, ((1, 1), (1, 1), (1, 1), (0, 0)))
    pieces = []
    for first in range(3):
        for second in range(3):
            for third in range(3):
                pieces.append(
                    padded[
                        first : first + edge : 2,
                        second : second + edge : 2,
                        third : third + edge : 2,
                    ]
                )
    pieces.append(values[0::2, 0::2, 0::2])
    return jnp.stack(pieces, axis=3).reshape(half * half * half, 28, width)


def spread_back(values, grad_rows, piece, half):
    width = piece.shape[1]
    edge = 2 * half
    grid = jnp.zeros((edge + 2, edge + 2, edge + 2, width), jnp.float32)
    for first in range(3):
        block = jnp.einsum(
            "qo,tco->qtc",
            grad_rows,
            piece[9 * first : 9 * first + 9],
            preferred_element_type=jnp.float32,
        )
        block = block.reshape(half, half, half, 9, width)
        for second in range(3):
            for third in range(3):
                grid = grid.at[
                    first : first + edge : 2, second : second + edge : 2, third : third + edge : 2
                ].add(block[:, :, :, 3 * second + third])
    direct = jnp.einsum(
        "qo,co->qc", grad_rows, piece[27], preferred_element_type=jnp.float32
    ).reshape(half, half, half, width)
    own = values.astype(jnp.float32)
    sigma = jax.nn.sigmoid(own)
    grad_in = grid[1:-1, 1:-1, 1:-1] * sigma * (1.0 + own * (1.0 - sigma))
    grad_in = grad_in.at[0::2, 0::2, 0::2].add(direct)
    return grad_in.astype(jnp.bfloat16)


def general(inputs, cotangent, weights):
    values = inputs[0]
    edge = values.shape[0]
    half = edge // 2
    chans = values.shape[3]
    cols = build_cols(values)
    grad_rows = cotangent[0].reshape(half * half * half, chans)
    result = jnp.einsum(
        "qtc,tco->qo",
        cols,
        lax.all_gather(weights, "shard", axis=1, tiled=True),
        preferred_element_type=jnp.float32,
    )
    grad_in = spread_back(
        values, grad_rows, lax.all_gather(weights, "shard", axis=1, tiled=True), half
    )
    group_values = lax.all_to_all(inputs, "shard", split_axis=4, concat_axis=0, tiled=True)
    group_grads = lax.all_gather(cotangent, "shard", axis=0, tiled=True)
    count = group_values.shape[0]
    group_cols = jax.vmap(build_cols)(group_values)
    group_rows = group_grads.reshape(count, half * half * half, chans)
    per_sample = jnp.einsum(
        "sqtc,sqo->stco", group_cols, group_rows, preferred_element_type=jnp.float32
    )
    owned = jnp.sum(per_sample.astype(jnp.bfloat16).astype(jnp.float32), axis=0)
    weight_grad = lax.psum(owned, "dp")
    outputs = result.astype(jnp.bfloat16).reshape(1, half, half, half, chans)
    return (outputs, grad_in.reshape(1, edge, edge, edge, chans), weight_grad)


def fits(mesh, inputs, cotangent, weights):
    groups_of, shards_of = mesh.shape["dp"], mesh.shape["shard"]
    edge, chans = inputs.shape[1], inputs.shape[4]
    ratio = groups_of // PARTS
    return (
        shards_of == 2
        and chans == shards_of * LANES
        and inputs.shape[0] == groups_of * shards_of
        and inputs.shape[1:4] == (8, 8, 8)
        and groups_of % PARTS == 0
        and ratio & (ratio - 1) == 0
    )


def solution(mesh):
    rows = P(("dp", "shard"), None, None, None, None)
    kernel = P(None, "shard", None)

    def whole(inputs, cotangent, weights):
        body = general
        if fits(mesh, inputs, cotangent, weights):
            body = functools.partial(shards, mesh.shape["dp"], mesh.shape["shard"])
        return jax.shard_map(
            body,
            mesh=mesh,
            in_specs=(rows, rows, kernel),
            out_specs=(rows, rows, kernel),
            check_vma=False,
        )(inputs, cotangent, weights)

    return whole
```
